512 devices in a mesh: gx: 32 (over z, x_lo), gy: 16 (over y, x_hi, core).
Axes of the slice: x: 4 (x_hi: 2, x_lo: 2; x = x_hi * 2 + x_lo), y: 4, z: 16, core: 2. Of those that a mesh axis runs over, the one named last changes fastest.
Arguments:
- cell_offset: float32 [3, 64, 32, 2048], P(None, 'gx', 'gy'), may hold values from 0 to 1
- velocity: float32 [3, 64, 32, 2048], P(None, 'gx', 'gy'), may hold values from -6 to 6
- affine: float32 [9, 64, 32, 2048], P(None, 'gx', 'gy'), may hold values from -3 to 3
- cell_index: int32 [64, 32, 2048], P('gx', 'gy'), may hold values from 0 to 63
- counts: int32 [64, 32, 32], P('gx', 'gy'), may hold values from 16 to 64, as said below
- cell_flags: int32 [256, 128, 128], P('gx', 'gy'), may hold values from 0 to 2, as said below
- old_pressure: float32 [256, 128, 128], P('gx', 'gy'), may hold values from -6 to 6
- destination: int32 [64, 32, 2048], P('gx', 'gy'), may hold values from 0 to 8, as said below
- dest_slot: int32 [64, 32, 2048], P('gx', 'gy'), may hold values from 0 to 255, as said below
Outputs:
- new_offset: float32 [3, 64, 32, 2048], P(None, 'gx', 'gy')
- new_velocity: float32 [3, 64, 32, 2048], P(None, 'gx', 'gy')
- new_affine: float32 [9, 64, 32, 2048], P(None, 'gx', 'gy')
- pressure: float32 [256, 128, 128], P('gx', 'gy')
- received: float32 [15, 8, 32, 4096], P(None, None, 'gx', 'gy')
The draws below stay inside these ranges and needn't reach their ends.
Inputs may be any that keep to these rules, and one draw needn't show every extreme that they name: `counts`: every block holds at least 16 live particles, and some block of every draw holds exactly 64. `cell_flags`: cell kinds: 0 air, 1 fluid, 2 solid. `destination`: only live particles move. From one box, between 64 and 256 particles move in each direction, and in every box exactly 256 move in some direction. `dest_slot`: particles of one box that move in one direction have distinct slots; for staying particles the value is meaningless.
All inputs are finite; a program needn't handle non-finite values.
Results may differ from the reference program's by a relative error of at most 0.0003.
Values sent between devices are 32-bit elements; how exact they have to be, the bound alone decides.
A program may use at most 64 MiB of HBM per device.

```python
import jax
import jax.numpy as jnp

CX = 8
CY = 8
NZ = 128
CAP = 64
MIG = 256
ITERS = 4
NX = 256
NY = 128
XB = 64
YB = 32
ZB = 32
N_GX = 32
N_GY = 16


def migration_plan(key):
    devices_x = NX // CX
    devices_y = NY // CY
    blocks_dev = CX // 4 * (CY // 4) * (NZ // 4)
    per_device = blocks_dev * CAP
    device_count = devices_x * devices_y
    keys = jax.random.split(jax.random.fold_in(key, 71), 7)
    device_top = jax.random.randint(keys[0], (device_count, 1), CAP // 2, CAP + 1)
    raw_counts = jax.random.randint(keys[1], (device_count, blocks_dev), 0, CAP + 1)
    block_counts = jnp.clip(jnp.minimum(raw_counts, device_top), CAP // 4, CAP)
    chosen = jax.random.randint(keys[2], (), 0, device_count * blocks_dev)
    block_counts = block_counts.reshape(-1).at[chosen].set(CAP).reshape(device_count, blocks_dev)
    per_direction = jax.random.randint(keys[3], (device_count, 8), MIG // 4, MIG + 1)
    full_direction = jax.random.randint(keys[4], (device_count, 1), 0, 8)
    per_direction = jnp.where(jnp.arange(8, dtype=jnp.int32)[None, :] == full_direction, MIG, per_direction)
    starts = jnp.cumsum(per_direction, axis=1) - per_direction
    moving_total = jnp.sum(per_direction, axis=1)
    slot_number = jnp.arange(per_device, dtype=jnp.int32) % CAP
    block_number = jnp.arange(per_device, dtype=jnp.int32) // CAP
    alive_mask = slot_number[None, :] < block_counts[:, block_number]
    orders = jax.vmap(lambda sub_key: jax.random.permutation(sub_key, per_device))(jax.random.split(keys[5], device_count))
    scores = orders.astype(jnp.int32) + (1 - alive_mask.astype(jnp.int32)) * per_device
    ranking = jnp.argsort(jnp.argsort(scores, axis=1), axis=1).astype(jnp.int32)
    direction_index = jnp.zeros_like(ranking)
    for number in range(1, 8):
        direction_index = direction_index + (ranking >= starts[:, number][:, None]).astype(jnp.int32)
    migrant = ranking < moving_total[:, None]
    start_of = jnp.take_along_axis(starts, direction_index, axis=1)
    filler = jax.random.randint(keys[6], (device_count, per_device), 0, MIG)
    destination = jnp.where(migrant, direction_index + 1, 0)
    slot_values = jnp.where(migrant, ranking - start_of, filler)

    def arrange(values, last):
        shaped = values.reshape(devices_x, devices_y, CX // 4, CY // 4, last)
        return shaped.transpose(0, 2, 1, 3, 4).reshape(devices_x * (CX // 4), devices_y * (CY // 4), last)
    return (arrange(block_counts, NZ // 4), arrange(destination, NZ // 4 * CAP), arrange(slot_values, NZ // 4 * CAP))


def draw_counts(key, part):
    return migration_plan(key)[0].astype(jnp.int32)


def draw_destination(key, part):
    return migration_plan(key)[1].astype(jnp.int32)


def draw_dest_slot(key, part):
    return migration_plan(key)[2].astype(jnp.int32)


def draw_cell_flags(key, part):
    key = jax.random.fold_in(key, 5)
    raw_kind = jax.random.randint(key, (NX, NY, NZ), 0, 10)
    return jnp.where(raw_kind < 6, 1, jnp.where(raw_kind < 8, 0, 2)).astype(jnp.int32)


def with_ends(array, key, smallest, high):
    extent = array.shape
    index_at = [jax.random.randint(jax.random.fold_in(key, axis), (), 0, extent[axis]) for axis in range(len(extent))]
    array = array.at[tuple(index_at)].set(smallest)
    longest = extent.index(max(extent))
    index_at[longest] = (index_at[longest] + 1) % extent[longest]
    return array.at[tuple(index_at)].set(high)


def steps_of(rng, shape, cuts, low, top_value):
    level, own = 1.0, jax.random.fold_in(rng, 6)
    for position, blocks in cuts:
        heights = jnp.exp(jax.random.uniform(jax.random.fold_in(own, position), (blocks,), jnp.float32, low / len(cuts), top_value / len(cuts)))
        level = level * jnp.repeat(heights, shape[position] // blocks).reshape([-1 if axis == position else 1 for axis in range(len(shape))])
    return level


def scatter_about(key, dims, spread, reach, shards=(), held_as=jnp.bfloat16):
    loudness = steps_of(key, dims, shards, -0.22, 0.18) if shards else 1.0
    result = jax.random.normal(key, dims, jnp.float32) * spread * loudness
    return jnp.minimum(jnp.maximum(result, -reach), reach).astype(held_as)


def setup_inputs(seed: int = 0) -> dict:
    seeds = jax.random.split(jax.random.key(seed), 10)
    cell_offset = jnp.clip(1.0 * jax.random.uniform(seeds[0], (3, XB, YB, ZB * CAP), jnp.float32) ** steps_of(seeds[0], (3, XB, YB, ZB * CAP), ((1, 32), (2, 16)), -0.2, 0.2), 0.0, 1.0)
    velocity = scatter_about(seeds[1], (3, XB, YB, ZB * CAP), 1.0, 6.0, ((1, 32), (2, 16)), jnp.float32)
    affine = scatter_about(seeds[2], (9, XB, YB, ZB * CAP), 0.5, 3.0, ((1, 32), (2, 16)), jnp.float32)
    cell_index = with_ends(jax.random.randint(seeds[3], (XB, YB, ZB * CAP), 0, 64), jax.random.fold_in(seeds[3], 1), 0, 63).astype(jnp.int32)
    counts = draw_counts(jax.random.fold_in(seeds[9], 71), 0)
    cell_flags = draw_cell_flags(jax.random.fold_in(seeds[9], 71), 0)
    old_pressure = scatter_about(seeds[6], (NX, NY, NZ), 1.0, 6.0, ((0, 32), (1, 16)), jnp.float32)
    destination = draw_destination(jax.random.fold_in(seeds[9], 71), 0)
    dest_slot = draw_dest_slot(jax.random.fold_in(seeds[9], 71), 0)
    return {"cell_offset": cell_offset, "velocity": velocity, "affine": affine, "cell_index": cell_index, "counts": counts, "cell_flags": cell_flags, "old_pressure": old_pressure, "destination": destination, "dest_slot": dest_slot}


corner_offsets = ((0, 0, 0), (0, 0, 1), (0, 1, 0), (0, 1, 1), (1, 0, 0), (1, 0, 1), (1, 1, 0), (1, 1, 1))
neighbour_steps = ((1, 0), (-1, 0), (0, 1), (0, -1), (1, 1), (1, -1), (-1, 1), (-1, -1))
time_step = 0.25
gravity = 1.0
mass_floor = 0.5


def corner_weights(offset, alive_mask):
    collected = []
    for corner in corner_offsets:
        factors = [offset[dimension] if corner[dimension] else 1.0 - offset[dimension] for dimension in range(3)]
        sign_terms = [1.0 if corner[dimension] else -1.0 for dimension in range(3)]
        weight = factors[0] * factors[1] * factors[2] * alive_mask
        gradient = [sign_terms[0] * factors[1] * factors[2] * alive_mask,
                    factors[0] * sign_terms[1] * factors[2] * alive_mask,
                    factors[0] * factors[1] * sign_terms[2] * alive_mask]
        collected.append((corner, weight, gradient))
    return collected


def neighbour_views(grid_field):
    padded = jnp.pad(grid_field, [(0, 0)] * (grid_field.ndim - 1) + [(1, 1)])
    return (padded[..., 2:, 1:-1, 1:-1], padded[..., :-2, 1:-1, 1:-1],
            padded[..., 1:-1, 2:, 1:-1], padded[..., 1:-1, :-2, 1:-1],
            padded[..., 1:-1, 1:-1, 2:], padded[..., 1:-1, 1:-1, :-2])


def crop(grid_field, layers):
    return grid_field[..., layers:grid_field.shape[-3] - layers, layers:grid_field.shape[-2] - layers, :]


def divergence(velocity_ext):
    neighbours = neighbour_views(velocity_ext)
    return 0.5 * ((neighbours[0][0] - neighbours[1][0]) + (neighbours[2][1] - neighbours[3][1])
                  + (neighbours[4][2] - neighbours[5][2]))


def jacobi_sweep(pressure_ext, flags_ext, source):
    pressure_sides = neighbour_views(pressure_ext)
    flag_sides = neighbour_views(flags_ext)
    neighbour_sum = jnp.zeros_like(source)
    open_count = jnp.zeros_like(source)
    for side_pressure, side_flag in zip(pressure_sides, flag_sides):
        open_side = side_flag != 2.0
        neighbour_sum = neighbour_sum + jnp.where(open_side, side_pressure, 0.0)
        open_count = open_count + open_side.astype(source.dtype)
    centre_flag = crop(flags_ext, 1)
    return jnp.where(centre_flag == 1.0, (neighbour_sum - source) / jnp.maximum(open_count, 1.0), 0.0)


def project(velocity_centre, pressure_ext, flags_ext):
    pressure_sides = neighbour_views(pressure_ext)
    flag_sides = neighbour_views(flags_ext)
    pressure_centre = crop(pressure_ext, 1)
    centre_flag = crop(flags_ext, 1)
    sided = [jnp.where(side_flag != 2.0, side_pressure, pressure_centre)
             for side_pressure, side_flag in zip(pressure_sides, flag_sides)]
    gradient = jnp.stack([0.5 * (sided[0] - sided[1]), 0.5 * (sided[2] - sided[3]), 0.5 * (sided[4] - sided[5])])
    return velocity_centre - jnp.where(centre_flag == 1.0, gradient, 0.0)


def padded_xy(grid_field):
    return jnp.pad(grid_field, [(0, 0)] * (grid_field.ndim - 3) + [(1, 1), (1, 1), (0, 0)])


def reference(cell_offset, velocity, affine, cell_index, counts, cell_flags, old_pressure, destination, dest_slot):
    block_shape = (XB, YB, ZB, CAP)
    float_type = cell_offset.dtype
    offset = cell_offset.reshape((3,) + block_shape)
    speeds = velocity.reshape((3,) + block_shape)
    matrix = affine.reshape((9,) + block_shape)
    cell_number = cell_index.reshape(block_shape)
    alive_mask = (jnp.arange(CAP, dtype=jnp.int32) < counts[..., None]).astype(float_type)
    cell_x = 4 * jnp.arange(XB, dtype=jnp.int32)[:, None, None, None] + cell_number // 16
    cell_y = 4 * jnp.arange(YB, dtype=jnp.int32)[None, :, None, None] + (cell_number // 4) % 4
    cell_z = 4 * jnp.arange(ZB, dtype=jnp.int32)[None, None, :, None] + cell_number % 4
    corners = corner_weights(offset, alive_mask)
    node_count = NX * NY * NZ
    node_mass = jnp.zeros((node_count,), float_type)
    momentum = jnp.zeros((3, node_count), float_type)
    for corner, weight, gradient in corners:
        node_x = cell_x + corner[0]
        node_y = cell_y + corner[1]
        node_z = cell_z + corner[2]
        inside = (node_x < NX) & (node_y < NY) & (node_z < NZ)
        target = jnp.where(inside, (node_x * NY + node_y) * NZ + node_z, node_count).astype(jnp.int32).reshape(-1)
        node_mass = node_mass.at[target].add(weight.reshape(-1), mode="drop")
        relative = [corner[dimension] - offset[dimension] for dimension in range(3)]
        for dimension in range(3):
            affine_term = (matrix[3 * dimension] * relative[0] + matrix[3 * dimension + 1] * relative[1]
                           + matrix[3 * dimension + 2] * relative[2])
            deposit = weight * (speeds[dimension] + affine_term)
            momentum = momentum.at[dimension, target].add(deposit.reshape(-1), mode="drop")
    node_mass = node_mass.reshape(NX, NY, NZ)
    momentum = momentum.reshape(3, NX, NY, NZ)
    flags_float = cell_flags.astype(float_type)
    grid_velocity = momentum / jnp.maximum(node_mass, mass_floor)
    grid_velocity = grid_velocity.at[2].add(-time_step * gravity)
    grid_velocity = jnp.where(cell_flags == 2, 0.0, grid_velocity)
    source = divergence(padded_xy(grid_velocity))
    pressure = jnp.where(cell_flags == 1, old_pressure, 0.0)
    flags_near = padded_xy(flags_float)
    for sweep_number in range(ITERS):
        pressure = jacobi_sweep(padded_xy(pressure), flags_near, source)
    settled = project(grid_velocity, padded_xy(pressure), flags_near)
    upper_nodes = jnp.pad(settled, ((0, 0), (0, 1), (0, 1), (0, 1)))
    new_speed = jnp.zeros_like(offset)
    new_matrix = [jnp.zeros_like(alive_mask) for entry in range(9)]
    for corner, weight, gradient in corners:
        sampled = upper_nodes[:, cell_x + corner[0], cell_y + corner[1], cell_z + corner[2]]
        new_speed = new_speed + weight[None] * sampled
        for row_axis in range(3):
            for column_axis in range(3):
                new_matrix[3 * row_axis + column_axis] = (new_matrix[3 * row_axis + column_axis]
                                                          + sampled[row_axis] * gradient[column_axis])
    new_offset = offset + time_step * new_speed
    box_x = cell_x // CX
    box_y = cell_y // CY
    step_x = jnp.zeros_like(destination.reshape(block_shape))
    step_y = jnp.zeros_like(step_x)
    moving = destination.reshape(block_shape)
    for number in range(8):
        step_x = step_x + (moving == number + 1).astype(jnp.int32) * neighbour_steps[number][0]
        step_y = step_y + (moving == number + 1).astype(jnp.int32) * neighbour_steps[number][1]
    receiver_x = box_x + step_x
    receiver_y = box_y + step_y
    valid = (moving > 0) & (receiver_x >= 0) & (receiver_x < N_GX) & (receiver_y >= 0) & (receiver_y < N_GY)
    buffer_size = 8 * N_GX * N_GY * MIG
    target = jnp.where(valid, (((moving - 1) * N_GX + receiver_x) * N_GY + receiver_y) * MIG
                       + dest_slot.reshape(block_shape), buffer_size).astype(jnp.int32).reshape(-1)
    rows = [(cell_x - receiver_x * CX).astype(float_type) + new_offset[0],
            (cell_y - receiver_y * CY).astype(float_type) + new_offset[1],
            cell_z.astype(float_type) + new_offset[2],
            new_speed[0], new_speed[1], new_speed[2]] + new_matrix
    received = jnp.stack([jnp.zeros((buffer_size,), float_type).at[target].set(row_values.reshape(-1), mode="drop")
                          for row_values in rows]).reshape(15, 8, N_GX, N_GY * MIG)
    return (new_offset.reshape(3, XB, YB, ZB * CAP), new_speed.reshape(3, XB, YB, ZB * CAP),
            jnp.stack(new_matrix).reshape(9, XB, YB, ZB * CAP), pressure, received)
```

```python
import functools

import jax
import jax.numpy as jnp
from jax import lax
from jax.experimental import pallas as pl
from jax.experimental.pallas import tpu as pltpu
from jax.sharding import PartitionSpec as P

F32, BF16, I32 = jnp.float32, jnp.bfloat16, jnp.int32
MESH = pl.DeviceIdType.MESH
STEPS = ((1, 0), (-1, 0), (0, 1), (0, -1), (1, 1), (1, -1), (-1, 1), (-1, -1))
TIME_STEP = 0.25
GRAVITY = 1.0
MASS_FLOOR = 0.5
ITERS = 4

WIDE_X = 19
FIELD_PARTS = (
    ((8, 13), (0, 5), 1),
    ((5, 11), (13, 19), 1),
    ((5, 13), (5, 13), 0),
    ((5, 13), (5, 13), 2),
    ((9, 13), (1, 5), 0),
    ((8, 13), (0, 5), 2),
    ((5, 10), (13, 18), 0),
    ((5, 11), (13, 19), 2),
)
SOURCE_PARTS = (
    ((9, 13), (1, 5), 1),
    ((5, 10), (13, 18), 1),
    ((5, 13), (5, 13), 0),
    ((5, 13), (5, 13), 2),
    ((10, 13), (2, 5), 0),
    ((9, 13), (1, 5), 2),
    ((5, 9), (13, 17), 0),
    ((5, 10), (13, 18), 2),
)
SUM_TILES = (9, 5, 9, 5, 2, 1, 1, 1)


def iota(shape, dim):
    return lax.broadcasted_iota(I32, shape, dim)


def below_z(v):
    axis = v.ndim - 1
    return jnp.where(iota(v.shape, axis) == 0, 0.0, pltpu.roll(v, 1, axis))


def above_z(v):
    axis = v.ndim - 1
    return jnp.where(iota(v.shape, axis) == 127, 0.0, pltpu.roll(v, 127, axis))


def two_parts(v):
    high = v.astype(BF16)
    return high, (v - high.astype(F32)).astype(BF16)


def dot_last(a, b):
    return lax.dot_general(a, b, (((1,), (1,)), ((), ())), preferred_element_type=F32)


def blocks_exchanged(parts):
    parts = list(parts)
    group = iota(parts[0].shape, 1) >> 3
    for bit in (1, 2, 4, 8):
        upper = (group & bit) != 0
        for i in range(16):
            if i & bit:
                continue
            low, high = parts[i], parts[i | bit]
            parts[i] = jnp.where(upper, pltpu.roll(high, 8 * bit, 1), low)
            parts[i | bit] = jnp.where(upper, high, pltpu.roll(low, 128 - 8 * bit, 1))
    return parts


def cell_row(x, y, ox, oy, k):
    return ((x + 1) * 10 + (y + 1)) * 16 + 8 * ox + 4 * oy + k


def kernel(
    nx,
    ny,
    off_h,
    vel_h,
    aff_h,
    cell_h,
    count_h,
    flag_h,
    press_h,
    dest_h,
    slot_h,
    off_o,
    vel_o,
    aff_o,
    press_o,
    rec_o,
    off_v,
    vel_v,
    aff_v,
    cell_v,
    count_v,
    dest_v,
    slot_v,
    flag_w,
    old_w,
    alive_v,
    bin_v,
    quant,
    binned,
    cells,
    nodes,
    column8,
    message0,
    message1,
    message2,
    message3,
    message4,
    message_d2,
    arrive0,
    arrive1,
    arrive2,
    arrive3,
    arrive4,
    arrive5,
    arrive6,
    arrive7,
    speed_w,
    source_w,
    scale_w,
    solid_w,
    press_a,
    press_b,
    settled,
    slot_onehot,
    parcels,
    records,
    outgoing,
    incoming,
    load_sem,
    send_sem,
    recv_sem,
):
    gx, gy = lax.axis_index("gx"), lax.axis_index("gy")
    where_x = {0: gx, 1: lax.rem(gx + 1, nx), -1: lax.rem(gx + nx - 1, nx)}
    where_y = {0: gy, 1: lax.rem(gy + 1, ny), -1: lax.rem(gy + ny - 1, ny)}
    inside_x = {0: gx >= 0, 1: gx < nx - 1, -1: gx > 0}
    inside_y = {0: gy >= 0, 1: gy < ny - 1, -1: gy > 0}

    def copy_to(number, stage, src, dst):
        dx, dy = STEPS[number]
        return pltpu.make_async_remote_copy(
            src_ref=src,
            dst_ref=dst,
            send_sem=send_sem.at[8 * stage + number],
            recv_sem=recv_sem.at[8 * stage + number],
            device_id=(where_x[dx], where_y[dy]),
            device_id_type=MESH,
        )

    own = (pl.ds(5, 8), pl.ds(8, 8))
    loads = [
        pltpu.make_async_copy(src, dst, load_sem.at[i])
        for i, (src, dst) in enumerate(
            (
                (flag_h, flag_w.at[own]),
                (press_h, old_w.at[own]),
                (count_h, count_v),
                (cell_h, cell_v),
                (off_h, off_v),
                (vel_h, vel_v),
                (aff_h, aff_v),
                (slot_h, slot_v),
                (dest_h, dest_v),
            )
        )
    ]
    for load in loads:
        load.start()

    barrier = pltpu.get_barrier_semaphore()
    for dx, dy in STEPS:
        pl.semaphore_signal(
            barrier, inc=1, device_id=(where_x[dx], where_y[dy]), device_id_type=MESH
        )

    zero_tile = jnp.zeros((8, 128), F32)
    for x in (0, 18):
        flag_w[x, 0:8] = jnp.zeros((8, 128), I32)
        old_w[x, 0:8] = zero_tile
    for x in range(WIDE_X):
        for field in (solid_w, press_a, press_b):
            field[x, 0:8] = zero_tile
            field[x, 32:40] = zero_tile
    for x in range(8):
        for half in (0, 8):
            cells[pl.ds(cell_row(x, -1, 0, 0, 0) + half, 8), :] = zero_tile
    for half in (0, 8):
        cells[pl.ds(cell_row(-1, 7, 0, 0, 0) + half, 8), :] = zero_tile

    pl.semaphore_wait(barrier, 8)
    loads[0].wait()
    loads[1].wait()

    exchanges = []
    for number in range(8):
        (s0, s1), (t0, t1), tile = FIELD_PARTS[number]
        for stage, field in ((0, flag_w), (1, old_w)):
            exchanges.append(
                copy_to(
                    number,
                    stage,
                    field.at[pl.ds(s0, s1 - s0), pl.ds(8, 8)],
                    field.at[pl.ds(t0, t1 - t0), pl.ds(8 * tile, 8)],
                )
            )
    for copy in exchanges:
        copy.start()

    for load in loads[2:7]:
        load.wait()

    sub32 = iota((32, 128), 0)
    lane32 = iota((32, 128), 1)
    for xb in range(2):
        r0 = 32 * xb
        row = iota((32, 32), 0)
        column = iota((32, 32), 1)
        totals = count_v[xb].astype(F32)
        spread = jnp.where(
            (row & 1) == 0,
            jnp.broadcast_to(totals[0:1], (32, 32)),
            jnp.broadcast_to(totals[1:2], (32, 32)),
        )
        spread = jnp.where((column >> 1) == (row >> 1), spread, 0.0).astype(BF16)
        half = ((sub32 & 1) == (lane32 >> 6)).astype(F32).astype(BF16)
        live = jnp.dot(spread, half, preferred_element_type=F32)
        alive_v[pl.ds(r0, 32), :] = jnp.where(
            (lane32 & 63).astype(F32) < live, 1.0, 0.0
        )
        number_in_block = cell_v[pl.ds(r0, 32), :]
        bin_v[pl.ds(r0, 32), :] = (
            ((number_in_block >> 2) << 3) + ((lane32 >> 6) << 2) + (number_in_block & 3)
        )

    def deposit(step, carry):
        rows = pl.ds(pl.multiple_of(step * 16, 16), 16)
        alive = alive_v[rows, :]
        f = [off_v[d, rows, :] for d in range(3)]
        a = [aff_v[j, rows, :] for j in range(9)]
        base = [
            vel_v[k, rows, :] - (a[3 * k] * f[0] + a[3 * k + 1] * f[1] + a[3 * k + 2] * f[2])
            for k in range(3)
        ]
        hx = [(1.0 - f[0]) * alive, f[0] * alive]
        hy = [1.0 - f[1], f[1]]
        hz = [1.0 - f[2], f[2]]
        for ox in range(2):
            bx = [base[k] + a[3 * k] if ox else base[k] for k in range(3)]
            for oy in range(2):
                by = [bx[k] + a[3 * k + 1] if oy else bx[k] for k in range(3)]
                hxy = hx[ox] * hy[oy]
                for oz in range(2):
                    w = hxy * hz[oz]
                    channel = 16 * oz + 8 * ox + 4 * oy
                    start = pl.multiple_of(channel * 64 + step * 16, 16)
                    quant[pl.ds(start, 16), :] = w
                    for k in range(3):
                        bz = by[k] + a[3 * k + 2] if oz else by[k]
                        start = pl.multiple_of((channel + k + 1) * 64 + step * 16, 16)
                        quant[pl.ds(start, 16), :] = w * bz
        return carry

    lax.fori_loop(0, 4, deposit, 0)

    def bin_column(col, carry):
        xb, yb = col // 2, lax.rem(col, 2)
        for zt in range(16):
            r = 32 * xb + yb + 2 * zt
            values = quant[pl.ds(r, 32, stride=64), :]
            high, low = two_parts(values)
            onehot = (
                (iota((128, 128), 0) == bin_v[pl.ds(r, 1), :]).astype(F32).astype(BF16)
            )
            total = dot_last(jnp.concatenate([high, low], axis=0), onehot)
            binned[zt] = total[0:32] + total[32:64]
        for g in range(2):
            lower = blocks_exchanged([binned[zt, 8 * g : 8 * g + 8] for zt in range(16)])
            upper = blocks_exchanged(
                [binned[zt, 16 + 8 * g : 24 + 8 * g] for zt in range(16)]
            )
            for q in range(16):
                start = ((4 * xb + q // 4 + 1) * 10 + 4 * yb + q % 4 + 1) * 16 + 8 * g
                cells[pl.ds(pl.multiple_of(start, 8), 8), :] = lower[q] + below_z(upper[q])
        return carry

    lax.fori_loop(0, 4, bin_column, 0)

    for k in range(4):
        for x in range(9):
            total = None
            for ox in range(2):
                if not 0 <= x - ox < 8:
                    continue
                for oy in range(2):
                    part = cells[pl.ds(cell_row(x - ox, -oy, ox, oy, k), 8, stride=16), :]
                    total = part if total is None else total + part
            nodes[pl.ds((k * 9 + x) * 8, 8), :] = total
        column8[k] = (
            cells[pl.ds(cell_row(0, 7, 0, 1, k), 8, stride=160), :]
            + cells[pl.ds(cell_row(-1, 7, 1, 1, k), 8, stride=160), :]
        )

    def four(x, y, ox, oy):
        return cells[pl.ds(cell_row(x, y, ox, oy, 0), 4), :]

    corner88 = four(7, 7, 1, 1)
    d1 = jnp.concatenate([corner88, four(0, 7, 0, 1)], axis=0)
    d2 = jnp.concatenate([four(7, 0, 1, 0), four(0, 0, 0, 0)], axis=0)
    d3 = jnp.concatenate(
        [four(7, 7, 0, 1) + four(6, 7, 1, 1), four(7, 7, 1, 0) + four(7, 6, 1, 1)], axis=0
    )
    for k in range(4):
        message0[2 * k] = nodes[pl.ds((k * 9 + 7) * 8, 8), :]
        message0[2 * k + 1] = nodes[pl.ds((k * 9 + 8) * 8, 8), :]
        message1[k] = nodes[pl.ds(k * 72, 8), :]
        message2[2 * k] = nodes[pl.ds(k * 72 + 7, 8, stride=8), :]
        message2[2 * k + 1] = column8[k]
        message3[k] = nodes[pl.ds(k * 72, 8, stride=8), :]
    message0[8] = d1
    message1[4] = d1
    message2[8] = d1
    message3[4] = d2
    message4[0] = d1
    message4[1] = d3
    message_d2[0] = d2

    sums = [
        copy_to(number, 2, src, dst)
        for number, src, dst in (
            (0, message0, arrive0),
            (1, message1, arrive1),
            (2, message2, arrive2),
            (3, message3, arrive3),
            (4, message4, arrive4),
            (5, message_d2, arrive5),
            (6, message4.at[pl.ds(0, 1)], arrive6),
            (7, message_d2, arrive7),
        )
    ]
    for copy in sums:
        copy.start()

    loads[7].wait()
    loads[8].wait()

    def slot_rows(step, carry):
        for j in range(4):
            r = 4 * step + j
            slot = jnp.where(dest_v[pl.ds(r, 1), :] > 0, slot_v[pl.ds(r, 1), :], -1)
            slot_onehot[:, pl.ds(pl.multiple_of(r * 128, 128), 128)] = (
                (iota((256, 128), 0) == slot).astype(F32).astype(BF16)
            )
        return carry

    for copy in exchanges:
        copy.wait_recv()

    sub24 = iota((24, 128), 0)
    ok_y = jnp.where(
        sub24 < 8,
        inside_y[-1].astype(I32),
        jnp.where(sub24 >= 16, inside_y[1].astype(I32), 1),
    )
    for x in range(WIDE_X):
        side = -1 if x < 5 else 1 if x >= 13 else 0
        kind = flag_w[x]
        kind = kind * ok_y
        if side:
            kind = kind * inside_x[side].astype(I32)
        solid_w[x, 8:32] = jnp.where(kind == 2, 1.0, 0.0)
        fluid = kind == 1
        scale_w[x] = jnp.where(fluid, 1.0, 0.0)
        press_a[x, 8:32] = jnp.where(fluid, old_w[x], 0.0)
    for x in range(1, WIDE_X - 1):
        middle = solid_w[x, 8:32]
        closed = (
            solid_w[x - 1, 8:32]
            + solid_w[x + 1, 8:32]
            + solid_w[x, 7:31]
            + solid_w[x, 9:33]
            + below_z(middle)
            + above_z(middle)
        )
        scale_w[x] = scale_w[x] / jnp.maximum(6.0 - closed, 1.0)

    lax.fori_loop(0, 8, slot_rows, 0)

    for copy in sums:
        copy.wait_recv()

    sub8 = iota((8, 128), 0)

    def kept(v, dx, dy):
        if dx:
            v = jnp.where(inside_x[dx], v, 0.0)
        if dy:
            v = jnp.where(inside_y[dy], v, 0.0)
        return v

    def at_first(v, row):
        return jnp.where(sub8 == 0, v + row, v)

    speed_f = speed_w.reshape(3 * 10 * 24, 128)
    flag_f = flag_w.reshape(WIDE_X * 24, 128)

    def normalised(sums4, kind, dx, dy):
        inverse = 1.0 / jnp.maximum(sums4[0], MASS_FLOOR)
        result = []
        for k in range(3):
            u = sums4[k + 1] * inverse
            if k == 2:
                u = u - TIME_STEP * GRAVITY
            result.append(kept(jnp.where(kind == 2, 0.0, u), dx, dy))
        return result

    minus_rows, zero_rows, plus_rows, below_columns, upper_columns = [], [], [], [], []
    for k in range(4):
        minus_rows.append(
            at_first(
                kept(arrive0[2 * k], -1, 0), kept(arrive4[1, k : k + 1], -1, -1)
            )
        )
        first = nodes[pl.ds(k * 72, 8), :] + kept(arrive0[2 * k + 1], -1, 0)
        nodes[pl.ds(k * 72, 8), :] = first
        column = at_first(
            kept(arrive2[2 * k + 1], 0, -1), kept(arrive4[0, k : k + 1], -1, -1)
        )
        nodes[pl.ds(k * 72, 8, stride=8), :] = (
            nodes[pl.ds(k * 72, 8, stride=8), :] + column
        )
        plus_rows.append(
            at_first(
                nodes[pl.ds((k * 9 + 8) * 8, 8), :] + kept(arrive1[k], 1, 0),
                kept(arrive2[8, k : k + 1], 0, -1)
                + kept(arrive6[0, 4 + k : 5 + k], 1, -1),
            )
        )
        below_columns.append(
            at_first(
                kept(arrive2[2 * k], 0, -1), kept(arrive4[1, 4 + k : 5 + k], -1, -1)
            )
        )
        upper_columns.append(
            at_first(
                column8[k] + kept(arrive3[k], 0, 1),
                kept(arrive0[8, k : k + 1], -1, 0) + kept(arrive5[0, k : k + 1], -1, 1),
            )
        )
    corner = (
        message4[0, 0:4]
        + kept(arrive1[4, 4:8], 1, 0)
        + kept(arrive3[4, 0:4], 0, 1)
        + kept(arrive7[0, 4:8], 1, 1)
    )

    for x in range(-1, 9):
        if x == -1:
            sums4, side = minus_rows, -1
        elif x == 8:
            sums4, side = plus_rows, 1
        else:
            sums4 = [nodes[pl.ds((k * 9 + x) * 8, 8), :] for k in range(4)]
            side = 0
        u = normalised(sums4, flag_w[x + 5, 8:16], side, 0)
        for k in range(3):
            speed_w[k, x + 1, 8:16] = u[k]
    for columns, y, side in ((below_columns, 7, -1), (upper_columns, 16, 1)):
        u = normalised(columns, flag_f[pl.ds(5 * 24 + y, 8, stride=24), :], 0, side)
        for k in range(3):
            speed_f[pl.ds((k * 10 + 1) * 24 + y, 8, stride=24), :] = u[k]
    u = normalised(
        [corner[k : k + 1] for k in range(4)], flag_w[13, 16:17], 1, 1
    )
    for k in range(3):
        speed_w[k, 9, 16:17] = u[k]

    for x in range(8):
        source_w[x + 5, 8:16] = 0.5 * (
            speed_w[0, x + 2, 8:16]
            - speed_w[0, x, 8:16]
            + (speed_w[1, x + 1, 9:17] - speed_w[1, x + 1, 7:15])
            + (above_z(speed_w[2, x + 1, 8:16]) - below_z(speed_w[2, x + 1, 8:16]))
        )

    margins = []
    for number in range(8):
        (s0, s1), (t0, t1), tile = SOURCE_PARTS[number]
        margins.append(
            copy_to(
                number,
                3,
                source_w.at[pl.ds(s0, s1 - s0), pl.ds(8, 8)],
                source_w.at[pl.ds(t0, t1 - t0), pl.ds(8 * tile, 8)],
            )
        )
    for copy in margins:
        copy.start()
    lax.fori_loop(8, 16, slot_rows, 0)
    for copy in margins:
        copy.wait_recv()

    old, new = press_a, press_b
    for sweep in range(ITERS):
        low, high = sweep + 1, WIDE_X - 1 - sweep
        for x in range(low, high):
            middle = old[x, 8:32]
            near = (
                old[x - 1, 8:32]
                + old[x + 1, 8:32]
                + old[x, 7:31]
                + old[x, 9:33]
                + below_z(middle)
                + above_z(middle)
            )
            scale = scale_w[x]
            new[x, 8:32] = jnp.where(scale > 0.0, scale * (near - source_w[x]), 0.0)
        old, new = new, old
    for x in range(8):
        press_o[x] = old[x + 5, 16:24]

    for x in range(9):
        w = x + 5
        p, s = old[w, 16:32], solid_w[w, 16:32]
        fluid = scale_w[w, 8:24] > 0.0
        slopes = (
            old[w + 1, 16:32]
            - old[w - 1, 16:32]
            + p * (solid_w[w + 1, 16:32] - solid_w[w - 1, 16:32]),
            old[w, 17:33]
            - old[w, 15:31]
            + p * (solid_w[w, 17:33] - solid_w[w, 15:31]),
            above_z(p) - below_z(p) + p * (above_z(s) - below_z(s)),
        )
        for k in range(3):
            settled[k, x] = speed_w[k, x + 1, 8:24] - jnp.where(fluid, 0.5 * slopes[k], 0.0)

    odd8 = (iota((8, 128), 0) & 1) == 1
    for xb in range(2):
        rows = pl.ds(32 * xb, 32)
        cell = cell_v[rows, :]
        alive = alive_v[rows, :]
        qx, qy = cell >> 4, (cell >> 2) & 3
        z = ((sub32 >> 1) << 3) + ((lane32 >> 6) << 2) + (cell & 3)
        f = [off_v[d, rows, :] for d in range(3)]
        speeds, offsets = [], []
        for k in range(3):
            pick_x = [[None] * 4, [None] * 4]
            for ix in range(5):
                pick_y = [[None] * 2, [None] * 2]
                for iy in range(5):
                    even = jnp.broadcast_to(settled[k, 4 * xb + ix, iy : iy + 1], (8, 128))
                    odd = jnp.broadcast_to(settled[k, 4 * xb + ix, iy + 4 : iy + 5], (8, 128))
                    table = jnp.where(odd8, odd, even)
                    rise = above_z(table) - table
                    got = [
                        jnp.take_along_axis(jnp.concatenate([t] * 4, axis=0), z, axis=1)
                        for t in (table, rise)
                    ]
                    for o in range(2):
                        if not 0 <= iy - o < 4:
                            continue
                        for j in range(2):
                            held = pick_y[o][j]
                            pick_y[o][j] = (
                                got[j]
                                if held is None
                                else jnp.where(qy == iy - o, got[j], held)
                            )
                flat = pick_y[0] + pick_y[1]
                for o in range(2):
                    if not 0 <= ix - o < 4:
                        continue
                    for j in range(4):
                        held = pick_x[o][j]
                        pick_x[o][j] = (
                            flat[j] if held is None else jnp.where(qx == ix - o, flat[j], held)
                        )
            value, along_y, along_z = [], [], []
            for o in range(2):
                a0, d0, a1, d1_ = pick_x[o]
                v0 = a0 + f[2] * d0
                v1 = a1 + f[2] * d1_
                along_y.append(v1 - v0)
                value.append(v0 + f[1] * (v1 - v0))
                along_z.append(d0 + f[1] * (d1_ - d0))
            along_x = value[1] - value[0]
            speed = (value[0] + f[0] * along_x) * alive
            offset = f[k] + TIME_STEP * speed
            speeds.append(speed)
            offsets.append(offset)
            slope = (
                along_x * alive,
                (along_y[0] + f[0] * (along_y[1] - along_y[0])) * alive,
                (along_z[0] + f[0] * (along_z[1] - along_z[0])) * alive,
            )
            off_o[k, rows, :] = offset
            vel_o[k, rows, :] = speed
            records[pl.ds((3 + k) * 64 + 32 * xb, 32), :] = speed
            for b in range(3):
                aff_o[3 * k + b, rows, :] = slope[b]
                records[pl.ds((6 + 3 * k + b) * 64 + 32 * xb, 32), :] = slope[b]
        moving = dest_v[rows, :]

        def one_of(*numbers):
            hit = moving == numbers[0]
            for number in numbers[1:]:
                hit = hit | (moving == number)
            return jnp.where(hit, 8, 0)

        place = (
            4 * xb + qx - one_of(1, 5, 6) + one_of(2, 7, 8),
            None,
            z,
        )
        row_y = (sub32 & 1) << 2
        place = (
            place[0],
            row_y + qy - one_of(3, 5, 7) + one_of(4, 6, 8),
            z,
        )
        for d in range(3):
            records[pl.ds(d * 64 + 32 * xb, 32), :] = place[d].astype(F32) + offsets[d]
        records[pl.ds(15 * 64 + 32 * xb, 32), :] = jnp.zeros((32, 128), F32)

    def parcel_rows(step, carry):
        for j in range(4):
            r = 4 * step + j
            record = records[pl.ds(r, 16, stride=64), :]
            high, low = two_parts(record)
            moving = jnp.broadcast_to(dest_v[pl.ds(r, 1), :], (16, 128))
            lanes = pl.ds(pl.multiple_of(r * 128, 128), 128)
            for number in range(8):
                picked = (moving == number + 1).astype(F32).astype(BF16)
                parcels[pl.ds(32 * number, 16), lanes] = high * picked
                parcels[pl.ds(32 * number + 16, 16), lanes] = low * picked
        return carry

    lax.fori_loop(0, 16, parcel_rows, 0)
    leaving = [None] * 8
    for half in (1, 0):
        placed = dot_last(parcels[pl.ds(128 * half, 128), :], slot_onehot[...])
        for j in range(4):
            number = 4 * half + j
            outgoing[number] = placed[32 * j : 32 * j + 16] + placed[32 * j + 16 : 32 * j + 32]
            leaving[number] = copy_to(number, 4, outgoing.at[number], incoming.at[number])
            leaving[number].start()

    for copy in exchanges + sums + margins:
        copy.wait_send()

    rec_f = rec_o.reshape(15 * 16, 128)
    for number in (4, 5, 6, 7, 0, 1, 2, 3):
        leaving[number].wait()
        dx, dy = STEPS[number]
        arrived = kept(incoming[number], -dx, -dy)
        for half in range(2):
            rec_f[pl.ds(2 * number + half, 15, stride=16), :] = arrived[
                0:15, 128 * half : 128 * half + 128
            ]


def in_rows(a):
    lead = a.shape[:-3]
    n = len(lead)
    turned = a.reshape(lead + (2, 2, 16, 128)).transpose(
        tuple(range(n)) + (n, n + 2, n + 1, n + 3)
    )
    return turned.reshape(lead + (64, 128))


def from_rows(a):
    lead = a.shape[:-2]
    n = len(lead)
    turned = a.reshape(lead + (2, 16, 2, 128)).transpose(
        tuple(range(n)) + (n, n + 2, n + 1, n + 3)
    )
    return turned.reshape(lead + (2, 2, 2048))


def on_device(
    nx,
    ny,
    cell_offset,
    velocity,
    affine,
    cell_index,
    counts,
    cell_flags,
    old_pressure,
    destination,
    dest_slot,
):
    vmem = pl.BlockSpec(memory_space=pltpu.VMEM)
    anywhere = pl.BlockSpec(memory_space=pltpu.HBM)

    def f32(*shape):
        return pltpu.VMEM(shape, F32)

    outs = pl.pallas_call(
        functools.partial(kernel, nx, ny),
        out_shape=[
            jax.ShapeDtypeStruct((3, 64, 128), F32),
            jax.ShapeDtypeStruct((3, 64, 128), F32),
            jax.ShapeDtypeStruct((9, 64, 128), F32),
            jax.ShapeDtypeStruct((8, 8, 128), F32),
            jax.ShapeDtypeStruct((15, 16, 128), F32),
        ],
        in_specs=[anywhere] * 9,
        out_specs=[vmem] * 5,
        scratch_shapes=[
            f32(3, 64, 128),
            f32(3, 64, 128),
            f32(9, 64, 128),
            pltpu.VMEM((64, 128), I32),
            pltpu.VMEM((2, 2, 32), I32),
            pltpu.VMEM((64, 128), I32),
            pltpu.VMEM((64, 128), I32),
            pltpu.VMEM((WIDE_X, 24, 128), I32),
            f32(WIDE_X, 24, 128),
            f32(64, 128),
            pltpu.VMEM((64, 128), I32),
            f32(32 * 64, 128),
            f32(16, 32, 128),
            f32(10 * 10 * 16, 128),
            f32(4 * 9 * 8, 128),
            f32(4, 8, 128),
            f32(9, 8, 128),
            f32(5, 8, 128),
            f32(9, 8, 128),
            f32(5, 8, 128),
            f32(2, 8, 128),
            f32(1, 8, 128),
        ]
        + [f32(tiles, 8, 128) for tiles in SUM_TILES]
        + [
            f32(3, 10, 24, 128),
            f32(WIDE_X, 24, 128),
            f32(WIDE_X, 24, 128),
            f32(WIDE_X, 40, 128),
            f32(WIDE_X, 40, 128),
            f32(WIDE_X, 40, 128),
            f32(3, 9, 16, 128),
            pltpu.VMEM((256, 8192), BF16),
            pltpu.VMEM((256, 8192), BF16),
            f32(16 * 64, 128),
            f32(8, 16, 256),
            f32(8, 16, 256),
            pltpu.SemaphoreType.DMA((9,)),
            pltpu.SemaphoreType.DMA((40,)),
            pltpu.SemaphoreType.DMA((40,)),
        ],
        compiler_params=pltpu.CompilerParams(
            collective_id=0, has_side_effects=True, vmem_limit_bytes=48 * 1024 * 1024
        ),
        name="substep",
    )(
        in_rows(cell_offset),
        in_rows(velocity),
        in_rows(affine),
        in_rows(cell_index),
        counts,
        cell_flags,
        old_pressure,
        in_rows(destination),
        in_rows(dest_slot),
    )
    return (
        from_rows(outs[0]),
        from_rows(outs[1]),
        from_rows(outs[2]),
        outs[3],
        outs[4].reshape(15, 8, 1, 256),
    )


def solution(mesh):
    particles, blocks = P(None, "gx", "gy", None), P("gx", "gy", None)
    return jax.shard_map(
        functools.partial(on_device, mesh.shape["gx"], mesh.shape["gy"]),
        mesh=mesh,
        in_specs=(particles, particles, particles) + (blocks,) * 6,
        out_specs=(particles, particles, particles, blocks, P(None, None, "gx", "gy")),
        check_vma=False,
    )
```

```python
import functools

import jax
import jax.numpy as jnp
from jax import lax
from jax.experimental import pallas as pl
from jax.experimental.pallas import tpu as pltpu
from jax.sharding import PartitionSpec as P

F32, BF16, I32 = jnp.float32, jnp.bfloat16, jnp.int32
MESH = pl.DeviceIdType.MESH
STEPS = ((1, 0), (-1, 0), (0, 1), (0, -1), (1, 1), (1, -1), (-1, 1), (-1, -1))
TIME_STEP = 0.25
GRAVITY = 1.0
MASS_FLOOR = 0.5
ITERS = 4

WIDE_X = 19
FIELD_REACH = ITERS + 1
SOURCE_REACH = ITERS


def corner_runs(number, reach):
    dx, dy = STEPS[number]
    runs = []
    for far in range(1, reach + 1) if dx > 0 else range(reach + 1):
        x = 8 - far if dx > 0 else far
        left = reach - far
        if dy > 0 and left > 0:
            runs.append((x, 8 - left, x - 8 * dx, -left, left))
        elif dy < 0:
            runs.append((x, 0, x - 8 * dx, 8, left + 1))
    return runs


def corner_tiles(number, reach):
    return -(-sum(run[4] for run in corner_runs(number, reach)) // 8)


SUM_TILES = (7, 5, 7, 5, 2, 1, 1, 1)


def iota(shape, dim):
    return lax.broadcasted_iota(I32, shape, dim)


def below_z(v):
    axis = v.ndim - 1
    return jnp.where(iota(v.shape, axis) == 0, 0.0, pltpu.roll(v, 1, axis))


def above_z(v):
    axis = v.ndim - 1
    return jnp.where(iota(v.shape, axis) == 127, 0.0, pltpu.roll(v, 127, axis))


def two_parts(v):
    high = v.astype(BF16)
    return high, (v - high.astype(F32)).astype(BF16)


def matches(row, count):
    places = iota((count, 128), 0).astype(F32).astype(BF16)
    wanted = jnp.broadcast_to(row.astype(F32), (count, 128)).astype(BF16)
    return jnp.where(places == wanted, 1.0, 0.0).astype(BF16)


def dot_last(a, b):
    return lax.dot_general(a, b, (((1,), (1,)), ((), ())), preferred_element_type=F32)


def blocks_exchanged(parts):
    parts = list(parts)
    group = iota(parts[0].shape, 1) >> 3
    for bit in (1, 2, 4, 8):
        upper = (group & bit) != 0
        for i in range(16):
            if i & bit:
                continue
            low, high = parts[i], parts[i | bit]
            parts[i] = jnp.where(upper, pltpu.roll(high, 8 * bit, 1), low)
            parts[i | bit] = jnp.where(upper, high, pltpu.roll(low, 128 - 8 * bit, 1))
    return parts


def cell_row(x, y, ox, oy, k):
    return ((x + 1) * 10 + (y + 1)) * 16 + 8 * ox + 4 * oy + k


def kernel(
    nx,
    ny,
    off_h,
    vel_h,
    aff_h,
    cell_h,
    count_h,
    flag_h,
    press_h,
    dest_h,
    slot_h,
    off_o,
    vel_o,
    aff_o,
    press_o,
    rec_o,
    off_v,
    vel_v,
    aff_v,
    cell_v,
    count_v,
    dest_v,
    slot_v,
    flag_v,
    field_w,
    alive_v,
    bin_v,
    quant,
    binned,
    cells,
    nodes,
    column8,
    message0,
    message1,
    message2,
    message3,
    message4,
    message_d2,
    arrive0,
    arrive1,
    arrive2,
    arrive3,
    arrive4,
    arrive5,
    arrive6,
    arrive7,
    field_out,
    field_in,
    source_out,
    source_in,
    speed_w,
    source_w,
    scale_w,
    solid_w,
    press_a,
    press_b,
    settled,
    tables,
    slot_onehot,
    parcels,
    records,
    outgoing,
    incoming,
    load_sem,
    send_sem,
    recv_sem,
):
    gx, gy = lax.axis_index("gx"), lax.axis_index("gy")
    where_x = {0: gx, 1: lax.rem(gx + 1, nx), -1: lax.rem(gx + nx - 1, nx)}
    where_y = {0: gy, 1: lax.rem(gy + 1, ny), -1: lax.rem(gy + ny - 1, ny)}
    inside_x = {0: gx >= 0, 1: gx < nx - 1, -1: gx > 0}
    inside_y = {0: gy >= 0, 1: gy < ny - 1, -1: gy > 0}

    def copy_to(number, stage, src, dst):
        dx, dy = STEPS[number]
        return pltpu.make_async_remote_copy(
            src_ref=src,
            dst_ref=dst,
            send_sem=send_sem.at[8 * stage + number],
            recv_sem=recv_sem.at[8 * stage + number],
            device_id=(where_x[dx], where_y[dy]),
            device_id_type=MESH,
        )

    def flat_rows(field):
        return field.reshape(field.shape[0] * WIDE_X * 24, 128)

    def halo(stage, field, outs, ins, reach):
        flat = flat_rows(field)
        lows, highs = reach, reach + 1
        copies = [
            copy_to(
                0,
                stage,
                field.at[:, pl.ds(13 - lows, lows), pl.ds(8, 8)],
                field.at[:, pl.ds(5 - lows, lows), pl.ds(8, 8)],
            ),
            copy_to(
                1,
                stage,
                field.at[:, pl.ds(5, highs), pl.ds(8, 8)],
                field.at[:, pl.ds(13, highs), pl.ds(8, 8)],
            ),
        ]
        for number in range(2, 8):
            out = outs[number - 2]
            for c in range(field.shape[0]):
                if number < 4:
                    first, columns = (8 - lows, lows) if number == 2 else (0, highs)
                    for j in range(columns):
                        start = (c * WIDE_X + 5) * 24 + 8 + first + j
                        out[c, pl.ds(8 * j, 8)] = flat[pl.ds(start, 8, stride=24), :]
                else:
                    row = 0
                    for x, y, _, _, length in corner_runs(number, reach):
                        out[c, row : row + length] = field[c, x + 5, y + 8 : y + 8 + length]
                        row += length
            copies.append(copy_to(number, stage, out, ins[number - 2]))
        return copies

    def unpack(field, ins, reach):
        flat = flat_rows(field)
        for number in range(2, 8):
            got = ins[number - 2]
            for c in range(field.shape[0]):
                if number < 4:
                    first, columns = (8 - reach, reach) if number == 2 else (16, reach + 1)
                    for j in range(columns):
                        start = (c * WIDE_X + 5) * 24 + first + j
                        flat[pl.ds(start, 8, stride=24), :] = got[c, pl.ds(8 * j, 8)]
                else:
                    row = 0
                    for _, _, x, y, length in corner_runs(number, reach):
                        field[c, x + 5, y + 8 : y + 8 + length] = got[c, row : row + length]
                        row += length

    def kept(v, dx, dy):
        if dx:
            v = jnp.where(inside_x[dx], v, 0.0)
        if dy:
            v = jnp.where(inside_y[dy], v, 0.0)
        return v

    own = (1, pl.ds(5, 8), pl.ds(8, 8))
    loads = [
        pltpu.make_async_copy(src, dst, load_sem.at[i])
        for i, (src, dst) in enumerate(
            (
                (flag_h, flag_v),
                (press_h, field_w.at[own]),
                (count_h, count_v),
                (cell_h, cell_v),
                (off_h, off_v),
                (vel_h, vel_v),
                (aff_h, aff_v),
                (slot_h, slot_v),
                (dest_h, dest_v),
            )
        )
    ]
    for load in loads:
        load.start()

    barrier = pltpu.get_barrier_semaphore()
    for dx, dy in STEPS:
        pl.semaphore_signal(
            barrier, inc=1, device_id=(where_x[dx], where_y[dy]), device_id_type=MESH
        )

    zero_tile = jnp.zeros((8, 128), F32)
    for x in range(WIDE_X):
        for field in (solid_w, press_a, press_b):
            field[x, 0:8] = zero_tile
            field[x, 32:40] = zero_tile
    for x in range(8):
        for half in (0, 8):
            cells[pl.ds(cell_row(x, -1, 0, 0, 0) + half, 8), :] = zero_tile
    for half in (0, 8):
        cells[pl.ds(cell_row(-1, 7, 0, 0, 0) + half, 8), :] = zero_tile

    pl.semaphore_wait(barrier, 8)
    loads[0].wait()
    loads[1].wait()

    for x in range(8):
        field_w[0, x + 5, 8:16] = flag_v[x].astype(F32)
    exchanges = halo(0, field_w, field_out, field_in, FIELD_REACH)
    for copy in exchanges:
        copy.start()

    for load in loads[2:7]:
        load.wait()

    sub32 = iota((32, 128), 0)
    lane32 = iota((32, 128), 1)
    for xb in range(2):
        r0 = 32 * xb
        row = iota((32, 32), 0)
        column = iota((32, 32), 1)
        totals = count_v[xb].astype(F32)
        spread = jnp.where(
            (row & 1) == 0,
            jnp.broadcast_to(totals[0:1], (32, 32)),
            jnp.broadcast_to(totals[1:2], (32, 32)),
        )
        spread = jnp.where((column >> 1) == (row >> 1), spread, 0.0).astype(BF16)
        half = ((sub32 & 1) == (lane32 >> 6)).astype(F32).astype(BF16)
        live = jnp.dot(spread, half, preferred_element_type=F32)
        alive_v[pl.ds(r0, 32), :] = jnp.where(
            (lane32 & 63).astype(F32) < live, 1.0, 0.0
        )
        number_in_block = cell_v[pl.ds(r0, 32), :]
        bin_v[pl.ds(r0, 32), :] = (
            ((number_in_block >> 2) << 3) + ((lane32 >> 6) << 2) + (number_in_block & 3)
        )

    def deposit(step, carry):
        rows = pl.ds(pl.multiple_of(step * 16, 16), 16)
        alive = alive_v[rows, :]
        f = [off_v[d, rows, :] for d in range(3)]
        a = [aff_v[j, rows, :] for j in range(9)]
        base = [
            vel_v[k, rows, :] - (a[3 * k] * f[0] + a[3 * k + 1] * f[1] + a[3 * k + 2] * f[2])
            for k in range(3)
        ]
        hx = [(1.0 - f[0]) * alive, f[0] * alive]
        hy = [1.0 - f[1], f[1]]
        hz = [1.0 - f[2], f[2]]
        for ox in range(2):
            bx = [base[k] + a[3 * k] if ox else base[k] for k in range(3)]
            for oy in range(2):
                by = [bx[k] + a[3 * k + 1] if oy else bx[k] for k in range(3)]
                hxy = hx[ox] * hy[oy]
                for oz in range(2):
                    w = hxy * hz[oz]
                    channel = 16 * oz + 8 * ox + 4 * oy
                    start = pl.multiple_of(channel * 64 + step * 16, 16)
                    quant[pl.ds(start, 16), :] = w
                    for k in range(3):
                        bz = by[k] + a[3 * k + 2] if oz else by[k]
                        start = pl.multiple_of((channel + k + 1) * 64 + step * 16, 16)
                        quant[pl.ds(start, 16), :] = w * bz
        return carry

    lax.fori_loop(0, 4, deposit, 0)

    def bin_column(col, carry):
        xb, yb = col // 2, lax.rem(col, 2)
        for zt in range(16):
            r = 32 * xb + yb + 2 * zt
            values = quant[pl.ds(r, 32, stride=64), :]
            high, low = two_parts(values)
            onehot = matches(bin_v[pl.ds(r, 1), :], 128)
            total = dot_last(jnp.concatenate([high, low], axis=0), onehot)
            binned[zt] = total[0:32] + total[32:64]
        first_z = (iota((8, 128), 1) & 7) == 0
        for g in range(2):
            parts = []
            for zt in range(16):
                same = pltpu.roll(binned[zt, 16 + 8 * g : 24 + 8 * g], 1, 1)
                before = (
                    pltpu.roll(binned[zt - 1, 16 + 8 * g : 24 + 8 * g], 121, 1) if zt else 0.0
                )
                parts.append(
                    binned[zt, 8 * g : 8 * g + 8] + jnp.where(first_z, before, same)
                )
            parts = blocks_exchanged(parts)
            for q in range(16):
                start = ((4 * xb + q // 4 + 1) * 10 + 4 * yb + q % 4 + 1) * 16 + 8 * g
                cells[pl.ds(pl.multiple_of(start, 8), 8), :] = parts[q]
        return carry

    lax.fori_loop(0, 4, bin_column, 0)

    for k in range(4):
        for x in range(9):
            total = None
            for ox in range(2):
                if not 0 <= x - ox < 8:
                    continue
                for oy in range(2):
                    part = cells[pl.ds(cell_row(x - ox, -oy, ox, oy, k), 8, stride=16), :]
                    total = part if total is None else total + part
            nodes[pl.ds((k * 9 + x) * 8, 8), :] = total
        column8[k] = (
            cells[pl.ds(cell_row(0, 7, 0, 1, k), 8, stride=160), :]
            + cells[pl.ds(cell_row(-1, 7, 1, 1, k), 8, stride=160), :]
        )

    def four(x, y, ox, oy):
        return cells[pl.ds(cell_row(x, y, ox, oy, 0), 4), :]

    corner88 = four(7, 7, 1, 1)
    d1 = jnp.concatenate([corner88, four(0, 7, 0, 1)], axis=0)
    d2 = jnp.concatenate([four(7, 0, 1, 0), four(0, 0, 0, 0)], axis=0)
    d3 = jnp.concatenate(
        [four(7, 7, 0, 1) + four(6, 7, 1, 1), four(7, 7, 1, 0) + four(7, 6, 1, 1)], axis=0
    )
    for k in range(4):
        message0[k] = nodes[pl.ds((k * 9 + 8) * 8, 8), :]
        message1[k] = nodes[pl.ds(k * 72, 8), :]
        message2[k] = column8[k]
        message3[k] = nodes[pl.ds(k * 72, 8, stride=8), :]
    for i, k in enumerate((0, 1)):
        message0[4 + i] = nodes[pl.ds((k * 9 + 7) * 8, 8), :]
    for i, k in enumerate((0, 2)):
        message2[4 + i] = nodes[pl.ds(k * 72 + 7, 8, stride=8), :]
    message0[6] = d1
    message1[4] = d1
    message2[6] = d1
    message3[4] = d2
    message4[0] = d1
    message4[1] = d3
    message_d2[0] = d2

    sums = [
        copy_to(number, 1, src, dst)
        for number, src, dst in (
            (0, message0, arrive0),
            (1, message1, arrive1),
            (2, message2, arrive2),
            (3, message3, arrive3),
            (4, message4, arrive4),
            (5, message_d2, arrive5),
            (6, message4.at[pl.ds(0, 1)], arrive6),
            (7, message_d2, arrive7),
        )
    ]
    for copy in sums:
        copy.start()

    loads[7].wait()
    loads[8].wait()

    def slot_rows(step, carry):
        for j in range(4):
            r = 4 * step + j
            slot = jnp.where(dest_v[pl.ds(r, 1), :] > 0, slot_v[pl.ds(r, 1), :], -1)
            lanes = pl.ds(pl.multiple_of(r * 128, 128), 128)
            slot_onehot[:, lanes] = matches(slot, 256)
        return carry

    for copy in exchanges:
        copy.wait_recv()
    unpack(field_w, field_in, FIELD_REACH)

    sub24 = iota((24, 128), 0)
    ok_y = (
        jnp.where(sub24 < 8, inside_y[-1].astype(I32), 1)
        * jnp.where(sub24 >= 16, inside_y[1].astype(I32), 1)
    ) > 0
    for x in range(WIDE_X):
        side = -1 if x < 5 else 1 if x >= 13 else 0
        kind = kept(jnp.where(ok_y, field_w[0, x], 0.0), side, 0)
        solid_w[x, 8:32] = jnp.where(kind == 2.0, 1.0, 0.0)
        fluid = kind == 1.0
        scale_w[x] = jnp.where(fluid, 1.0, 0.0)
        press_a[x, 8:32] = jnp.where(fluid, field_w[1, x], 0.0)
    for x in range(1, WIDE_X - 1):
        middle = solid_w[x, 8:32]
        closed = (
            solid_w[x - 1, 8:32]
            + solid_w[x + 1, 8:32]
            + solid_w[x, 7:31]
            + solid_w[x, 9:33]
            + below_z(middle)
            + above_z(middle)
        )
        scale_w[x] = scale_w[x] / jnp.maximum(6.0 - closed, 1.0)

    lax.fori_loop(0, 8, slot_rows, 0)

    for copy in sums:
        copy.wait_recv()

    sub8 = iota((8, 128), 0)

    def at_first(v, row):
        return jnp.where(sub8 == 0, v + row, v)

    speed_f = speed_w.reshape(3 * 10 * 24, 128)
    field_f = flat_rows(field_w)

    def normalised(sums4, kind, dx, dy, components=(0, 1, 2)):
        inverse = 1.0 / jnp.maximum(sums4[0], MASS_FLOOR)
        result = []
        for k in components:
            u = sums4[k + 1] * inverse
            if k == 2:
                u = u - TIME_STEP * GRAVITY
            result.append(kept(jnp.where(kind == 2.0, 0.0, u), dx, dy))
        return result

    minus_rows, below_columns = [None] * 4, [None] * 4
    for i, k in enumerate((0, 1)):
        minus_rows[k] = at_first(
            kept(arrive0[4 + i], -1, 0), kept(arrive4[1, k : k + 1], -1, -1)
        )
    for i, k in enumerate((0, 2)):
        below_columns[k] = at_first(
            kept(arrive2[4 + i], 0, -1), kept(arrive4[1, 4 + k : 5 + k], -1, -1)
        )
    plus_rows, upper_columns = [], []
    for k in range(4):
        first = nodes[pl.ds(k * 72, 8), :] + kept(arrive0[k], -1, 0)
        nodes[pl.ds(k * 72, 8), :] = first
        column = at_first(
            kept(arrive2[k], 0, -1), kept(arrive4[0, k : k + 1], -1, -1)
        )
        nodes[pl.ds(k * 72, 8, stride=8), :] = (
            nodes[pl.ds(k * 72, 8, stride=8), :] + column
        )
        plus_rows.append(
            at_first(
                nodes[pl.ds((k * 9 + 8) * 8, 8), :] + kept(arrive1[k], 1, 0),
                kept(arrive2[6, k : k + 1], 0, -1)
                + kept(arrive6[0, 4 + k : 5 + k], 1, -1),
            )
        )
        upper_columns.append(
            at_first(
                column8[k] + kept(arrive3[k], 0, 1),
                kept(arrive0[6, k : k + 1], -1, 0) + kept(arrive5[0, k : k + 1], -1, 1),
            )
        )
    corner = (
        message4[0, 0:4]
        + kept(arrive1[4, 4:8], 1, 0)
        + kept(arrive3[4, 0:4], 0, 1)
        + kept(arrive7[0, 4:8], 1, 1)
    )

    for x in range(-1, 9):
        if x == -1:
            sums4, side = minus_rows, -1
        elif x == 8:
            sums4, side = plus_rows, 1
        else:
            sums4 = [nodes[pl.ds((k * 9 + x) * 8, 8), :] for k in range(4)]
            side = 0
        wanted = (0,) if x == -1 else (0, 1, 2)
        u = normalised(sums4, field_w[0, x + 5, 8:16], side, 0, wanted)
        for k in wanted:
            speed_w[k, x + 1, 8:16] = u[k]
    for columns, y, side, wanted in (
        (below_columns, 7, -1, (1,)),
        (upper_columns, 16, 1, (0, 1, 2)),
    ):
        kind = field_f[pl.ds(5 * 24 + y, 8, stride=24), :]
        u = normalised(columns, kind, 0, side, wanted)
        for i, k in enumerate(wanted):
            speed_f[pl.ds((k * 10 + 1) * 24 + y, 8, stride=24), :] = u[i]
    u = normalised([corner[k : k + 1] for k in range(4)], field_w[0, 13, 16:17], 1, 1)
    for k in range(3):
        speed_w[k, 9, 16:17] = u[k]

    for x in range(8):
        source_w[0, x + 5, 8:16] = 0.5 * (
            speed_w[0, x + 2, 8:16]
            - speed_w[0, x, 8:16]
            + (speed_w[1, x + 1, 9:17] - speed_w[1, x + 1, 7:15])
            + (above_z(speed_w[2, x + 1, 8:16]) - below_z(speed_w[2, x + 1, 8:16]))
        )

    margins = halo(2, source_w, source_out, source_in, SOURCE_REACH)
    for copy in margins:
        copy.start()
    lax.fori_loop(8, 16, slot_rows, 0)
    for copy in margins:
        copy.wait_recv()
    unpack(source_w, source_in, SOURCE_REACH)

    old, new = press_a, press_b
    for sweep in range(ITERS):
        low, high = sweep + 1, WIDE_X - 1 - sweep
        for x in range(low, high):
            middle = old[x, 8:32]
            near = (
                old[x - 1, 8:32]
                + old[x + 1, 8:32]
                + old[x, 7:31]
                + old[x, 9:33]
                + below_z(middle)
                + above_z(middle)
            )
            scale = scale_w[x]
            new[x, 8:32] = jnp.where(scale > 0.0, scale * (near - source_w[0, x]), 0.0)
        old, new = new, old
    for x in range(8):
        press_o[x] = old[x + 5, 16:24]

    for x in range(9):
        w = x + 5
        p, s = old[w, 16:32], solid_w[w, 16:32]
        fluid = scale_w[w, 8:24] > 0.0
        slopes = (
            old[w + 1, 16:32]
            - old[w - 1, 16:32]
            + p * (solid_w[w + 1, 16:32] - solid_w[w - 1, 16:32]),
            old[w, 17:33]
            - old[w, 15:31]
            + p * (solid_w[w, 17:33] - solid_w[w, 15:31]),
            above_z(p) - below_z(p) + p * (above_z(s) - below_z(s)),
        )
        for k in range(3):
            settled[k, x] = speed_w[k, x + 1, 8:24] - jnp.where(fluid, 0.5 * slopes[k], 0.0)

    odd8 = (iota((8, 128), 0) & 1) == 1
    sub8 = iota((8, 128), 0)
    lane8 = iota((8, 128), 1)

    def table_row(k, ix, iy, j):
        return pl.ds(8 * (((k * 5 + ix) * 5 + iy) * 2 + j), 8)

    def sample_blocks(xb, carry):
        for k in range(3):
            for ix in range(5):
                for iy in range(5):
                    even = jnp.broadcast_to(settled[k, 4 * xb + ix, iy : iy + 1], (8, 128))
                    odd = jnp.broadcast_to(settled[k, 4 * xb + ix, iy + 4 : iy + 5], (8, 128))
                    table = jnp.where(odd8, odd, even)
                    tables[table_row(k, ix, iy, 0), :] = table
                    tables[table_row(k, ix, iy, 1), :] = above_z(table) - table
        return lax.fori_loop(0, 4, functools.partial(sample_rows, xb), carry)

    def sample_rows(xb, g, carry):
        start = pl.multiple_of(32 * xb + 8 * g, 8)
        rows = pl.ds(start, 8)
        cell = cell_v[rows, :]
        alive = alive_v[rows, :]
        qx, qy = cell >> 4, (cell >> 2) & 3
        z = ((4 * g + (sub8 >> 1)) << 3) + ((lane8 >> 6) << 2) + (cell & 3)
        at_x = [qx == i for i in range(4)]
        at_y = [qy == i for i in range(4)]
        f = [off_v[d, rows, :] for d in range(3)]

        def record_row(number):
            return pl.ds(pl.multiple_of(number * 64 + start, 8), 8)

        moving = dest_v[rows, :]

        def one_of(*numbers):
            hit = moving == numbers[0]
            for number in numbers[1:]:
                hit = hit | (moving == number)
            return jnp.where(hit, 8, 0)

        place = (
            4 * xb + qx - one_of(1, 5, 6) + one_of(2, 7, 8),
            ((sub8 & 1) << 2) + qy - one_of(3, 5, 7) + one_of(4, 6, 8),
            z,
        )
        for k in range(3):
            pick_x = [[None] * 4, [None] * 4]
            for ix in range(5):
                pick_y = [[None] * 2, [None] * 2]
                for iy in range(5):
                    got = [
                        jnp.take_along_axis(tables[table_row(k, ix, iy, j), :], z, axis=1)
                        for j in range(2)
                    ]
                    for o in range(2):
                        if not 0 <= iy - o < 4:
                            continue
                        for j in range(2):
                            held = pick_y[o][j]
                            pick_y[o][j] = (
                                got[j]
                                if held is None
                                else jnp.where(at_y[iy - o], got[j], held)
                            )
                flat = pick_y[0] + pick_y[1]
                for o in range(2):
                    if not 0 <= ix - o < 4:
                        continue
                    for j in range(4):
                        held = pick_x[o][j]
                        pick_x[o][j] = (
                            flat[j] if held is None else jnp.where(at_x[ix - o], flat[j], held)
                        )
            value, along_y, along_z = [], [], []
            for o in range(2):
                a0, rise0, a1, rise1 = pick_x[o]
                v0 = a0 + f[2] * rise0
                v1 = a1 + f[2] * rise1
                along_y.append(v1 - v0)
                value.append(v0 + f[1] * (v1 - v0))
                along_z.append(rise0 + f[1] * (rise1 - rise0))
            along_x = value[1] - value[0]
            speed = (value[0] + f[0] * along_x) * alive
            offset = f[k] + TIME_STEP * speed
            slope = (
                along_x * alive,
                (along_y[0] + f[0] * (along_y[1] - along_y[0])) * alive,
                (along_z[0] + f[0] * (along_z[1] - along_z[0])) * alive,
            )
            off_o[k, rows, :] = offset
            vel_o[k, rows, :] = speed
            records[record_row(k), :] = place[k].astype(F32) + offset
            records[record_row(3 + k), :] = speed
            for b in range(3):
                aff_o[3 * k + b, rows, :] = slope[b]
                records[record_row(6 + 3 * k + b), :] = slope[b]
        records[record_row(15), :] = jnp.zeros((8, 128), F32)
        return carry

    lax.fori_loop(0, 2, sample_blocks, 0)

    def parcel_rows(step, carry):
        for j in range(4):
            r = 4 * step + j
            record = records[pl.ds(r, 16, stride=64), :]
            high, low = two_parts(record)
            moving = jnp.broadcast_to(dest_v[pl.ds(r, 1), :].astype(F32), (16, 128)).astype(BF16)
            lanes = pl.ds(pl.multiple_of(r * 128, 128), 128)
            for number in range(8):
                hit = moving == number + 1
                parcels[pl.ds(32 * number, 16), lanes] = jnp.where(hit, high, 0.0).astype(BF16)
                parcels[pl.ds(32 * number + 16, 16), lanes] = jnp.where(hit, low, 0.0).astype(BF16)
        return carry

    lax.fori_loop(0, 16, parcel_rows, 0)
    placed = dot_last(parcels[...], slot_onehot[...])
    leaving = [None] * 8
    for number in (4, 5, 6, 7, 0, 1, 2, 3):
        first = 32 * number
        outgoing[number] = placed[first : first + 16] + placed[first + 16 : first + 32]
        leaving[number] = copy_to(number, 3, outgoing.at[number], incoming.at[number])
        leaving[number].start()

    for copy in exchanges + sums + margins:
        copy.wait_send()

    rec_f = rec_o.reshape(15 * 16, 128)
    for number in (4, 5, 6, 7, 0, 1, 2, 3):
        leaving[number].wait()
        dx, dy = STEPS[number]
        arrived = kept(incoming[number], -dx, -dy)
        for half in range(2):
            rec_f[pl.ds(2 * number + half, 15, stride=16), :] = arrived[
                0:15, 128 * half : 128 * half + 128
            ]


def write_out(*refs):
    copies = [
        pltpu.make_async_copy(refs[i], refs[5 + i], refs[10].at[i]) for i in range(5)
    ]
    for copy in copies:
        copy.start()
    for copy in copies:
        copy.wait()


def in_rows(a):
    lead = a.shape[:-3]
    n = len(lead)
    turned = a.reshape(lead + (2, 2, 16, 128)).transpose(
        tuple(range(n)) + (n, n + 2, n + 1, n + 3)
    )
    return turned.reshape(lead + (64, 128))


def from_rows(a):
    lead = a.shape[:-2]
    n = len(lead)
    turned = a.reshape(lead + (2, 16, 2, 128)).transpose(
        tuple(range(n)) + (n, n + 2, n + 1, n + 3)
    )
    return turned.reshape(lead + (2, 2, 2048))


def on_device(
    nx,
    ny,
    cell_offset,
    velocity,
    affine,
    cell_index,
    counts,
    cell_flags,
    old_pressure,
    destination,
    dest_slot,
):
    vmem = pl.BlockSpec(memory_space=pltpu.VMEM)
    anywhere = pl.BlockSpec(memory_space=pltpu.HBM)

    def f32(*shape):
        return pltpu.VMEM(shape, F32)

    def halos(count, reach):
        rows = [8 * reach, 8 * (reach + 1)] + [8 * corner_tiles(n, reach) for n in range(4, 8)]
        return [f32(count, n, 128) for n in rows]

    shapes = ((3, 64, 128), (3, 64, 128), (9, 64, 128), (8, 8, 128), (15, 16, 128))
    outs = pl.pallas_call(
        functools.partial(kernel, nx, ny),
        out_shape=[pltpu.VMEM(shape, F32) for shape in shapes],
        in_specs=[anywhere] * 9,
        out_specs=[vmem] * 5,
        scratch_shapes=[
            f32(3, 64, 128),
            f32(3, 64, 128),
            f32(9, 64, 128),
            pltpu.VMEM((64, 128), I32),
            pltpu.VMEM((2, 2, 32), I32),
            pltpu.VMEM((64, 128), I32),
            pltpu.VMEM((64, 128), I32),
            pltpu.VMEM((8, 8, 128), I32),
            f32(2, WIDE_X, 24, 128),
            f32(64, 128),
            pltpu.VMEM((64, 128), I32),
            f32(32 * 64, 128),
            f32(16, 32, 128),
            f32(10 * 10 * 16, 128),
            f32(4 * 9 * 8, 128),
            f32(4, 8, 128),
            f32(7, 8, 128),
            f32(5, 8, 128),
            f32(7, 8, 128),
            f32(5, 8, 128),
            f32(2, 8, 128),
            f32(1, 8, 128),
        ]
        + [f32(tiles, 8, 128) for tiles in SUM_TILES]
        + [
            halos(2, FIELD_REACH),
            halos(2, FIELD_REACH),
            halos(1, SOURCE_REACH),
            halos(1, SOURCE_REACH),
            f32(3, 10, 24, 128),
            f32(1, WIDE_X, 24, 128),
            f32(WIDE_X, 24, 128),
            f32(WIDE_X, 40, 128),
            f32(WIDE_X, 40, 128),
            f32(WIDE_X, 40, 128),
            f32(3, 9, 16, 128),
            f32(150 * 8, 128),
            pltpu.VMEM((256, 8192), BF16),
            pltpu.VMEM((256, 8192), BF16),
            f32(16 * 64, 128),
            f32(8, 16, 256),
            f32(8, 16, 256),
            pltpu.SemaphoreType.DMA((9,)),
            pltpu.SemaphoreType.DMA((32,)),
            pltpu.SemaphoreType.DMA((32,)),
        ],
        compiler_params=pltpu.CompilerParams(
            collective_id=0, has_side_effects=True, vmem_limit_bytes=60 * 1024 * 1024
        ),
        name="substep",
    )(
        *[
            pltpu.with_memory_space_constraint(a, pltpu.HBM)
            for a in (
                in_rows(cell_offset),
                in_rows(velocity),
                in_rows(affine),
                in_rows(cell_index),
                counts,
                cell_flags,
                old_pressure,
                in_rows(destination),
                in_rows(dest_slot),
            )
        ]
    )
    outs = pl.pallas_call(
        write_out,
        out_shape=[jax.ShapeDtypeStruct(shape, F32) for shape in shapes],
        in_specs=[vmem] * 5,
        out_specs=[anywhere] * 5,
        scratch_shapes=[pltpu.SemaphoreType.DMA((5,))],
        compiler_params=pltpu.CompilerParams(vmem_limit_bytes=60 * 1024 * 1024),
        name="write_out",
    )(*[pltpu.with_memory_space_constraint(a, pltpu.VMEM) for a in outs])
    return (
        from_rows(outs[0]),
        from_rows(outs[1]),
        from_rows(outs[2]),
        outs[3],
        outs[4].reshape(15, 8, 1, 256),
    )


def solution(mesh):
    particles, blocks = P(None, "gx", "gy", None), P("gx", "gy", None)
    return jax.shard_map(
        functools.partial(on_device, mesh.shape["gx"], mesh.shape["gy"]),
        mesh=mesh,
        in_specs=(particles, particles, particles) + (blocks,) * 6,
        out_specs=(particles, particles, particles, blocks, P(None, None, "gx", "gy")),
        check_vma=False,
    )
```

```python
import functools

import jax
import jax.numpy as jnp
from jax import lax
from jax.experimental import pallas as pl
from jax.experimental.pallas import tpu as pltpu
from jax.sharding import PartitionSpec as P

F32, BF16, I32 = jnp.float32, jnp.bfloat16, jnp.int32
MESH = pl.DeviceIdType.MESH
STEPS = ((1, 0), (-1, 0), (0, 1), (0, -1), (1, 1), (1, -1), (-1, 1), (-1, -1))
TIME_STEP = 0.25
GRAVITY = 1.0
MASS_FLOOR = 0.5
ITERS = 4

WIDE_X = 19
FIELD_REACH = ITERS + 1
SOURCE_REACH = ITERS


def corner_runs(number, reach):
    dx, dy = STEPS[number]
    runs = []
    for far in range(1, reach + 1) if dx > 0 else range(reach + 1):
        x = 8 - far if dx > 0 else far
        left = reach - far
        if dy > 0 and left > 0:
            runs.append((x, 8 - left, x - 8 * dx, -left, left))
        elif dy < 0:
            runs.append((x, 0, x - 8 * dx, 8, left + 1))
    return runs


def corner_tiles(number, reach):
    return -(-sum(run[4] for run in corner_runs(number, reach)) // 8)


SUM_TILES = (7, 5, 7, 5, 2, 1, 1, 1)


def iota(shape, dim):
    return lax.broadcasted_iota(I32, shape, dim)


def below_z(v):
    axis = v.ndim - 1
    return jnp.where(iota(v.shape, axis) == 0, 0.0, pltpu.roll(v, 1, axis))


def above_z(v):
    axis = v.ndim - 1
    return jnp.where(iota(v.shape, axis) == 127, 0.0, pltpu.roll(v, 127, axis))


def two_parts(v):
    high = v.astype(BF16)
    return high, (v - high.astype(F32)).astype(BF16)


def matches(row, count):
    places = iota((count, 128), 0).astype(F32).astype(BF16)
    wanted = jnp.broadcast_to(row.astype(F32), (count, 128)).astype(BF16)
    one, zero = jnp.ones((count, 128), BF16), jnp.zeros((count, 128), BF16)
    return jnp.where(places == wanted, one, zero)


def dot_last(a, b):
    return lax.dot_general(a, b, (((1,), (1,)), ((), ())), preferred_element_type=F32)


def blocks_exchanged(parts):
    parts = list(parts)
    group = iota(parts[0].shape, 1) >> 3
    for bit in (1, 2, 4, 8):
        upper = (group & bit) != 0
        for i in range(16):
            if i & bit:
                continue
            low, high = parts[i], parts[i | bit]
            parts[i] = jnp.where(upper, pltpu.roll(high, 8 * bit, 1), low)
            parts[i | bit] = jnp.where(upper, high, pltpu.roll(low, 128 - 8 * bit, 1))
    return parts


def cell_row(x, y, ox, oy, k):
    return ((x + 1) * 10 + (y + 1)) * 16 + 8 * ox + 4 * oy + k


class Neighbourly:
    def __init__(self, copy, goes, comes):
        self.copy, self.goes, self.comes = copy, goes, comes

    def start(self):
        pl.when(self.goes)(self.copy.start)

    def wait_send(self):
        pl.when(self.goes)(self.copy.wait_send)

    def wait_recv(self):
        pl.when(self.comes)(self.copy.wait_recv)


def kernel(
    nx,
    ny,
    off_h,
    vel_h,
    aff_h,
    cell_h,
    count_h,
    flag_h,
    press_h,
    dest_h,
    slot_h,
    off_o,
    vel_o,
    aff_o,
    press_o,
    rec_o,
    off_v,
    vel_v,
    aff_v,
    cell_v,
    count_v,
    dest_v,
    slot_v,
    flag_v,
    field_w,
    alive_v,
    bin_v,
    quant,
    binned,
    cells,
    nodes,
    column8,
    message0,
    message1,
    message2,
    message3,
    message4,
    message_d2,
    arrive0,
    arrive1,
    arrive2,
    arrive3,
    arrive4,
    arrive5,
    arrive6,
    arrive7,
    field_out,
    field_in,
    source_out,
    source_in,
    speed_w,
    source_w,
    scale_w,
    solid_w,
    press_a,
    press_b,
    settled,
    tables,
    slot_onehot,
    parcels,
    records,
    outgoing,
    incoming,
    load_sem,
    send_sem,
    recv_sem,
):
    gx, gy = lax.axis_index("gx"), lax.axis_index("gy")
    where_x = {0: gx, 1: lax.rem(gx + 1, nx), -1: lax.rem(gx + nx - 1, nx)}
    where_y = {0: gy, 1: lax.rem(gy + 1, ny), -1: lax.rem(gy + ny - 1, ny)}
    inside_x = {0: gx >= 0, 1: gx < nx - 1, -1: gx > 0}
    inside_y = {0: gy >= 0, 1: gy < ny - 1, -1: gy > 0}

    def copy_to(number, stage, src, dst):
        dx, dy = STEPS[number]
        copy = pltpu.make_async_remote_copy(
            src_ref=src,
            dst_ref=dst,
            send_sem=send_sem.at[8 * stage + number],
            recv_sem=recv_sem.at[8 * stage + number],
            device_id=(where_x[dx], where_y[dy]),
            device_id_type=MESH,
        )
        goes = inside_x[dx] & inside_y[dy]
        comes = inside_x[-dx] & inside_y[-dy]
        return Neighbourly(copy, goes, comes)

    def flat_rows(field):
        return field.reshape(field.shape[0] * WIDE_X * 24, 128)

    def halo(stage, field, outs, ins, reach):
        flat = flat_rows(field)
        lows, highs = reach, reach + 1
        copies = [
            copy_to(
                0,
                stage,
                field.at[:, pl.ds(13 - lows, lows), pl.ds(8, 8)],
                field.at[:, pl.ds(5 - lows, lows), pl.ds(8, 8)],
            ),
            copy_to(
                1,
                stage,
                field.at[:, pl.ds(5, highs), pl.ds(8, 8)],
                field.at[:, pl.ds(13, highs), pl.ds(8, 8)],
            ),
        ]
        for number in range(2, 8):
            out = outs[number - 2]
            for c in range(field.shape[0]):
                if number < 4:
                    first, columns = (8 - lows, lows) if number == 2 else (0, highs)
                    for j in range(columns):
                        start = (c * WIDE_X + 5) * 24 + 8 + first + j
                        out[c, pl.ds(8 * j, 8)] = flat[pl.ds(start, 8, stride=24), :]
                else:
                    row = 0
                    for x, y, _, _, length in corner_runs(number, reach):
                        out[c, row : row + length] = field[c, x + 5, y + 8 : y + 8 + length]
                        row += length
            copies.append(copy_to(number, stage, out, ins[number - 2]))
        return copies

    def unpack(field, ins, reach):
        flat = flat_rows(field)
        for number in range(2, 8):
            got = ins[number - 2]
            for c in range(field.shape[0]):
                if number < 4:
                    first, columns = (8 - reach, reach) if number == 2 else (16, reach + 1)
                    for j in range(columns):
                        start = (c * WIDE_X + 5) * 24 + first + j
                        flat[pl.ds(start, 8, stride=24), :] = got[c, pl.ds(8 * j, 8)]
                else:
                    row = 0
                    for _, _, x, y, length in corner_runs(number, reach):
                        field[c, x + 5, y + 8 : y + 8 + length] = got[c, row : row + length]
                        row += length

    def kept(v, dx, dy):
        if dx:
            v = jnp.where(inside_x[dx], v, 0.0)
        if dy:
            v = jnp.where(inside_y[dy], v, 0.0)
        return v

    own = (1, pl.ds(5, 8), pl.ds(8, 8))
    loads = [
        pltpu.make_async_copy(src, dst, load_sem.at[i])
        for i, (src, dst) in enumerate(
            (
                (flag_h, flag_v),
                (press_h, field_w.at[own]),
                (count_h, count_v),
                (cell_h, cell_v),
                (off_h, off_v),
                (vel_h, vel_v),
                (aff_h, aff_v),
                (slot_h, slot_v),
                (dest_h, dest_v),
            )
        )
    ]
    for load in loads:
        load.start()

    barrier = pltpu.get_barrier_semaphore()
    for dx, dy in STEPS:
        pl.when(inside_x[dx] & inside_y[dy])(
            functools.partial(
                pl.semaphore_signal,
                barrier,
                inc=1,
                device_id=(where_x[dx], where_y[dy]),
                device_id_type=MESH,
            )
        )
    near_x = 1 + inside_x[1].astype(I32) + inside_x[-1].astype(I32)
    near_y = 1 + inside_y[1].astype(I32) + inside_y[-1].astype(I32)

    zero_tile = jnp.zeros((8, 128), F32)
    for x in range(WIDE_X):
        for field in (solid_w, press_a, press_b):
            field[x, 0:8] = zero_tile
            field[x, 32:40] = zero_tile
    for x in range(8):
        for half in (0, 8):
            cells[pl.ds(cell_row(x, -1, 0, 0, 0) + half, 8), :] = zero_tile
    for half in (0, 8):
        cells[pl.ds(cell_row(-1, 7, 0, 0, 0) + half, 8), :] = zero_tile

    pl.semaphore_wait(barrier, near_x * near_y - 1)
    loads[0].wait()
    loads[1].wait()

    for x in range(8):
        field_w[0, x + 5, 8:16] = flag_v[x].astype(F32)
    exchanges = halo(0, field_w, field_out, field_in, FIELD_REACH)
    for copy in exchanges:
        copy.start()

    for load in loads[2:7]:
        load.wait()

    sub32 = iota((32, 128), 0)
    lane32 = iota((32, 128), 1)
    for xb in range(2):
        r0 = 32 * xb
        row = iota((32, 32), 0)
        column = iota((32, 32), 1)
        totals = count_v[xb].astype(F32)
        spread = jnp.where(
            (row & 1) == 0,
            jnp.broadcast_to(totals[0:1], (32, 32)),
            jnp.broadcast_to(totals[1:2], (32, 32)),
        )
        spread = jnp.where((column >> 1) == (row >> 1), spread, 0.0).astype(BF16)
        half = ((sub32 & 1) == (lane32 >> 6)).astype(F32).astype(BF16)
        live = jnp.dot(spread, half, preferred_element_type=F32)
        alive_v[pl.ds(r0, 32), :] = jnp.where(
            (lane32 & 63).astype(F32) < live, 1.0, 0.0
        )
        number_in_block = cell_v[pl.ds(r0, 32), :]
        bin_v[pl.ds(r0, 32), :] = (
            ((number_in_block >> 2) << 3) + ((lane32 >> 6) << 2) + (number_in_block & 3)
        )

    def deposit(step, carry):
        rows = pl.ds(pl.multiple_of(step * 16, 16), 16)
        alive = alive_v[rows, :]
        f = [off_v[d, rows, :] for d in range(3)]
        a = [aff_v[j, rows, :] for j in range(9)]
        base = [
            vel_v[k, rows, :] - (a[3 * k] * f[0] + a[3 * k + 1] * f[1] + a[3 * k + 2] * f[2])
            for k in range(3)
        ]
        hx = [(1.0 - f[0]) * alive, f[0] * alive]
        hy = [1.0 - f[1], f[1]]
        hz = [1.0 - f[2], f[2]]
        for ox in range(2):
            bx = [base[k] + a[3 * k] if ox else base[k] for k in range(3)]
            for oy in range(2):
                by = [bx[k] + a[3 * k + 1] if oy else bx[k] for k in range(3)]
                hxy = hx[ox] * hy[oy]
                for oz in range(2):
                    w = hxy * hz[oz]
                    channel = 16 * oz + 8 * ox + 4 * oy
                    start = pl.multiple_of(channel * 64 + step * 16, 16)
                    quant[pl.ds(start, 16), :] = w
                    for k in range(3):
                        bz = by[k] + a[3 * k + 2] if oz else by[k]
                        start = pl.multiple_of((channel + k + 1) * 64 + step * 16, 16)
                        quant[pl.ds(start, 16), :] = w * bz
        return carry

    lax.fori_loop(0, 4, deposit, 0)

    def bin_column(col, carry):
        xb, yb = col // 2, lax.rem(col, 2)
        for zt in range(16):
            r = 32 * xb + yb + 2 * zt
            values = quant[pl.ds(r, 32, stride=64), :]
            high, low = two_parts(values)
            onehot = matches(bin_v[pl.ds(r, 1), :], 128)
            total = dot_last(jnp.concatenate([high, low], axis=0), onehot)
            binned[zt] = total[0:32] + total[32:64]
        first_z = (iota((8, 128), 1) & 7) == 0
        for g in range(2):
            parts = []
            for zt in range(16):
                same = pltpu.roll(binned[zt, 16 + 8 * g : 24 + 8 * g], 1, 1)
                before = (
                    pltpu.roll(binned[zt - 1, 16 + 8 * g : 24 + 8 * g], 121, 1) if zt else 0.0
                )
                parts.append(
                    binned[zt, 8 * g : 8 * g + 8] + jnp.where(first_z, before, same)
                )
            parts = blocks_exchanged(parts)
            for q in range(16):
                start = ((4 * xb + q // 4 + 1) * 10 + 4 * yb + q % 4 + 1) * 16 + 8 * g
                cells[pl.ds(pl.multiple_of(start, 8), 8), :] = parts[q]
        return carry

    lax.fori_loop(0, 4, bin_column, 0)

    for k in range(4):
        for x in range(9):
            total = None
            for ox in range(2):
                if not 0 <= x - ox < 8:
                    continue
                for oy in range(2):
                    part = cells[pl.ds(cell_row(x - ox, -oy, ox, oy, k), 8, stride=16), :]
                    total = part if total is None else total + part
            nodes[pl.ds((k * 9 + x) * 8, 8), :] = total
        column8[k] = (
            cells[pl.ds(cell_row(0, 7, 0, 1, k), 8, stride=160), :]
            + cells[pl.ds(cell_row(-1, 7, 1, 1, k), 8, stride=160), :]
        )

    def four(x, y, ox, oy):
        return cells[pl.ds(cell_row(x, y, ox, oy, 0), 4), :]

    corner88 = four(7, 7, 1, 1)
    d1 = jnp.concatenate([corner88, four(0, 7, 0, 1)], axis=0)
    d2 = jnp.concatenate([four(7, 0, 1, 0), four(0, 0, 0, 0)], axis=0)
    d3 = jnp.concatenate(
        [four(7, 7, 0, 1) + four(6, 7, 1, 1), four(7, 7, 1, 0) + four(7, 6, 1, 1)], axis=0
    )
    for k in range(4):
        message0[k] = nodes[pl.ds((k * 9 + 8) * 8, 8), :]
        message1[k] = nodes[pl.ds(k * 72, 8), :]
        message2[k] = column8[k]
        message3[k] = nodes[pl.ds(k * 72, 8, stride=8), :]
    for i, k in enumerate((0, 1)):
        message0[4 + i] = nodes[pl.ds((k * 9 + 7) * 8, 8), :]
    for i, k in enumerate((0, 2)):
        message2[4 + i] = nodes[pl.ds(k * 72 + 7, 8, stride=8), :]
    message0[6] = d1
    message1[4] = d1
    message2[6] = d1
    message3[4] = d2
    message4[0] = d1
    message4[1] = d3
    message_d2[0] = d2

    sums = [
        copy_to(number, 1, src, dst)
        for number, src, dst in (
            (0, message0, arrive0),
            (1, message1, arrive1),
            (2, message2, arrive2),
            (3, message3, arrive3),
            (4, message4, arrive4),
            (5, message_d2, arrive5),
            (6, message4.at[pl.ds(0, 1)], arrive6),
            (7, message_d2, arrive7),
        )
    ]
    for copy in sums:
        copy.start()

    loads[7].wait()
    loads[8].wait()

    def slot_rows(step, carry):
        for j in range(4):
            r = 4 * step + j
            slot = jnp.where(dest_v[pl.ds(r, 1), :] > 0, slot_v[pl.ds(r, 1), :], -1)
            lanes = pl.ds(pl.multiple_of(r * 128, 128), 128)
            slot_onehot[:, lanes] = matches(slot, 256)
        return carry

    for copy in exchanges:
        copy.wait_recv()
    unpack(field_w, field_in, FIELD_REACH)

    sub24 = iota((24, 128), 0)
    ok_y = (
        jnp.where(sub24 < 8, inside_y[-1].astype(I32), 1)
        * jnp.where(sub24 >= 16, inside_y[1].astype(I32), 1)
    ) > 0
    for x in range(WIDE_X):
        side = -1 if x < 5 else 1 if x >= 13 else 0
        kind = kept(jnp.where(ok_y, field_w[0, x], 0.0), side, 0)
        solid_w[x, 8:32] = jnp.where(kind == 2.0, 1.0, 0.0)
        fluid = kind == 1.0
        scale_w[x] = jnp.where(fluid, 1.0, 0.0)
        press_a[x, 8:32] = jnp.where(fluid, field_w[1, x], 0.0)
    for x in range(1, WIDE_X - 1):
        middle = solid_w[x, 8:32]
        closed = (
            solid_w[x - 1, 8:32]
            + solid_w[x + 1, 8:32]
            + solid_w[x, 7:31]
            + solid_w[x, 9:33]
            + below_z(middle)
            + above_z(middle)
        )
        scale_w[x] = scale_w[x] / jnp.maximum(6.0 - closed, 1.0)

    lax.fori_loop(0, 8, slot_rows, 0)

    for copy in sums:
        copy.wait_recv()

    sub8 = iota((8, 128), 0)

    def at_first(v, row):
        return jnp.where(sub8 == 0, v + row, v)

    speed_f = speed_w.reshape(3 * 10 * 24, 128)
    field_f = flat_rows(field_w)

    def normalised(sums4, kind, dx, dy, components=(0, 1, 2)):
        inverse = 1.0 / jnp.maximum(sums4[0], MASS_FLOOR)
        result = []
        for k in components:
            u = sums4[k + 1] * inverse
            if k == 2:
                u = u - TIME_STEP * GRAVITY
            result.append(kept(jnp.where(kind == 2.0, 0.0, u), dx, dy))
        return result

    minus_rows, below_columns = [None] * 4, [None] * 4
    for i, k in enumerate((0, 1)):
        minus_rows[k] = at_first(
            kept(arrive0[4 + i], -1, 0), kept(arrive4[1, k : k + 1], -1, -1)
        )
    for i, k in enumerate((0, 2)):
        below_columns[k] = at_first(
            kept(arrive2[4 + i], 0, -1), kept(arrive4[1, 4 + k : 5 + k], -1, -1)
        )
    plus_rows, upper_columns = [], []
    for k in range(4):
        first = nodes[pl.ds(k * 72, 8), :] + kept(arrive0[k], -1, 0)
        nodes[pl.ds(k * 72, 8), :] = first
        column = at_first(
            kept(arrive2[k], 0, -1), kept(arrive4[0, k : k + 1], -1, -1)
        )
        nodes[pl.ds(k * 72, 8, stride=8), :] = (
            nodes[pl.ds(k * 72, 8, stride=8), :] + column
        )
        plus_rows.append(
            at_first(
                nodes[pl.ds((k * 9 + 8) * 8, 8), :] + kept(arrive1[k], 1, 0),
                kept(arrive2[6, k : k + 1], 0, -1)
                + kept(arrive6[0, 4 + k : 5 + k], 1, -1),
            )
        )
        upper_columns.append(
            at_first(
                column8[k] + kept(arrive3[k], 0, 1),
                kept(arrive0[6, k : k + 1], -1, 0) + kept(arrive5[0, k : k + 1], -1, 1),
            )
        )
    corner = (
        message4[0, 0:4]
        + kept(arrive1[4, 4:8], 1, 0)
        + kept(arrive3[4, 0:4], 0, 1)
        + kept(arrive7[0, 4:8], 1, 1)
    )

    for x in range(-1, 9):
        if x == -1:
            sums4, side = minus_rows, -1
        elif x == 8:
            sums4, side = plus_rows, 1
        else:
            sums4 = [nodes[pl.ds((k * 9 + x) * 8, 8), :] for k in range(4)]
            side = 0
        wanted = (0,) if x == -1 else (0, 1, 2)
        u = normalised(sums4, field_w[0, x + 5, 8:16], side, 0, wanted)
        for k in wanted:
            speed_w[k, x + 1, 8:16] = u[k]
    for columns, y, side, wanted in (
        (below_columns, 7, -1, (1,)),
        (upper_columns, 16, 1, (0, 1, 2)),
    ):
        kind = field_f[pl.ds(5 * 24 + y, 8, stride=24), :]
        u = normalised(columns, kind, 0, side, wanted)
        for i, k in enumerate(wanted):
            speed_f[pl.ds((k * 10 + 1) * 24 + y, 8, stride=24), :] = u[i]
    u = normalised([corner[k : k + 1] for k in range(4)], field_w[0, 13, 16:17], 1, 1)
    for k in range(3):
        speed_w[k, 9, 16:17] = u[k]

    for x in range(8):
        source_w[0, x + 5, 8:16] = 0.5 * (
            speed_w[0, x + 2, 8:16]
            - speed_w[0, x, 8:16]
            + (speed_w[1, x + 1, 9:17] - speed_w[1, x + 1, 7:15])
            + (above_z(speed_w[2, x + 1, 8:16]) - below_z(speed_w[2, x + 1, 8:16]))
        )

    margins = halo(2, source_w, source_out, source_in, SOURCE_REACH)
    for copy in margins:
        copy.start()
    lax.fori_loop(8, 16, slot_rows, 0)
    for copy in margins:
        copy.wait_recv()
    unpack(source_w, source_in, SOURCE_REACH)

    old, new = press_a, press_b
    for sweep in range(ITERS):
        low, high = sweep + 1, WIDE_X - 1 - sweep
        for x in range(low, high):
            middle = old[x, 8:32]
            near = (
                old[x - 1, 8:32]
                + old[x + 1, 8:32]
                + old[x, 7:31]
                + old[x, 9:33]
                + below_z(middle)
                + above_z(middle)
            )
            scale = scale_w[x]
            new[x, 8:32] = jnp.where(scale > 0.0, scale * (near - source_w[0, x]), 0.0)
        old, new = new, old
    for x in range(8):
        press_o[x] = old[x + 5, 16:24]

    for x in range(9):
        w = x + 5
        p, s = old[w, 16:32], solid_w[w, 16:32]
        fluid = scale_w[w, 8:24] > 0.0
        slopes = (
            old[w + 1, 16:32]
            - old[w - 1, 16:32]
            + p * (solid_w[w + 1, 16:32] - solid_w[w - 1, 16:32]),
            old[w, 17:33]
            - old[w, 15:31]
            + p * (solid_w[w, 17:33] - solid_w[w, 15:31]),
            above_z(p) - below_z(p) + p * (above_z(s) - below_z(s)),
        )
        for k in range(3):
            settled[k, x] = speed_w[k, x + 1, 8:24] - jnp.where(fluid, 0.5 * slopes[k], 0.0)

    odd8 = (iota((8, 128), 0) & 1) == 1
    sub8 = iota((8, 128), 0)
    lane8 = iota((8, 128), 1)

    def table_row(k, ix, iy, j):
        return pl.ds(8 * (((k * 5 + ix) * 5 + iy) * 2 + j), 8)

    def sample_blocks(xb, carry):
        for k in range(3):
            for ix in range(5):
                for iy in range(5):
                    even = jnp.broadcast_to(settled[k, 4 * xb + ix, iy : iy + 1], (8, 128))
                    odd = jnp.broadcast_to(settled[k, 4 * xb + ix, iy + 4 : iy + 5], (8, 128))
                    table = jnp.where(odd8, odd, even)
                    tables[table_row(k, ix, iy, 0), :] = table
                    tables[table_row(k, ix, iy, 1), :] = above_z(table) - table
        return lax.fori_loop(0, 4, functools.partial(sample_rows, xb), carry)

    def sample_rows(xb, g, carry):
        start = pl.multiple_of(32 * xb + 8 * g, 8)
        rows = pl.ds(start, 8)
        cell = cell_v[rows, :]
        alive = alive_v[rows, :]
        qx, qy = cell >> 4, (cell >> 2) & 3
        z = ((4 * g + (sub8 >> 1)) << 3) + ((lane8 >> 6) << 2) + (cell & 3)
        at_x = [qx == i for i in range(4)]
        at_y = [qy == i for i in range(4)]
        f = [off_v[d, rows, :] for d in range(3)]

        def record_row(number):
            return pl.ds(pl.multiple_of(number * 64 + start, 8), 8)

        moving = dest_v[rows, :]

        def one_of(*numbers):
            hit = moving == numbers[0]
            for number in numbers[1:]:
                hit = hit | (moving == number)
            return jnp.where(hit, 8, 0)

        place = (
            4 * xb + qx - one_of(1, 5, 6) + one_of(2, 7, 8),
            ((sub8 & 1) << 2) + qy - one_of(3, 5, 7) + one_of(4, 6, 8),
            z,
        )
        for k in range(3):
            pick_x = [[None] * 4, [None] * 4]
            for ix in range(5):
                pick_y = [[None] * 2, [None] * 2]
                for iy in range(5):
                    got = [
                        jnp.take_along_axis(tables[table_row(k, ix, iy, j), :], z, axis=1)
                        for j in range(2)
                    ]
                    for o in range(2):
                        if not 0 <= iy - o < 4:
                            continue
                        for j in range(2):
                            held = pick_y[o][j]
                            pick_y[o][j] = (
                                got[j]
                                if held is None
                                else jnp.where(at_y[iy - o], got[j], held)
                            )
                flat = pick_y[0] + pick_y[1]
                for o in range(2):
                    if not 0 <= ix - o < 4:
                        continue
                    for j in range(4):
                        held = pick_x[o][j]
                        pick_x[o][j] = (
                            flat[j] if held is None else jnp.where(at_x[ix - o], flat[j], held)
                        )
            value, along_y, along_z = [], [], []
            for o in range(2):
                a0, rise0, a1, rise1 = pick_x[o]
                v0 = a0 + f[2] * rise0
                v1 = a1 + f[2] * rise1
                along_y.append(v1 - v0)
                value.append(v0 + f[1] * (v1 - v0))
                along_z.append(rise0 + f[1] * (rise1 - rise0))
            along_x = value[1] - value[0]
            speed = (value[0] + f[0] * along_x) * alive
            offset = f[k] + TIME_STEP * speed
            slope = (
                along_x * alive,
                (along_y[0] + f[0] * (along_y[1] - along_y[0])) * alive,
                (along_z[0] + f[0] * (along_z[1] - along_z[0])) * alive,
            )
            off_o[k, rows, :] = offset
            vel_o[k, rows, :] = speed
            records[record_row(k), :] = place[k].astype(F32) + offset
            records[record_row(3 + k), :] = speed
            for b in range(3):
                aff_o[3 * k + b, rows, :] = slope[b]
                records[record_row(6 + 3 * k + b), :] = slope[b]
        records[record_row(15), :] = jnp.zeros((8, 128), F32)
        return carry

    lax.fori_loop(0, 2, sample_blocks, 0)

    def parcel_rows(step, carry):
        for j in range(4):
            r = 4 * step + j
            record = records[pl.ds(r, 16, stride=64), :]
            high, low = two_parts(record)
            both = jnp.concatenate([high, low], axis=0)
            moving = jnp.broadcast_to(dest_v[pl.ds(r, 1), :].astype(F32), (32, 128)).astype(BF16)
            lanes = pl.ds(pl.multiple_of(r * 128, 128), 128)
            for number in range(8):
                hit = moving == jnp.full((32, 128), number + 1, BF16)
                parcels[pl.ds(32 * number, 32), lanes] = jnp.where(hit, both, jnp.zeros_like(both))
        return carry

    lax.fori_loop(0, 16, parcel_rows, 0)
    placed = dot_last(parcels[...], slot_onehot[...])
    leaving = [None] * 8
    for number in (4, 5, 6, 7, 0, 1, 2, 3):
        first = 32 * number
        outgoing[number] = placed[first : first + 16] + placed[first + 16 : first + 32]
        leaving[number] = copy_to(number, 3, outgoing.at[number], incoming.at[number])
        leaving[number].start()

    for copy in exchanges + sums + margins:
        copy.wait_send()

    rec_f = rec_o.reshape(15 * 16, 128)
    for number in (4, 5, 6, 7, 0, 1, 2, 3):
        leaving[number].wait_recv()
        leaving[number].wait_send()
        dx, dy = STEPS[number]
        arrived = kept(incoming[number], -dx, -dy)
        for half in range(2):
            rec_f[pl.ds(2 * number + half, 15, stride=16), :] = arrived[
                0:15, 128 * half : 128 * half + 128
            ]


def write_out(*refs):
    copies = [
        pltpu.make_async_copy(refs[i], refs[5 + i], refs[10].at[i]) for i in range(5)
    ]
    for copy in copies:
        copy.start()
    for copy in copies:
        copy.wait()


def in_rows(a):
    lead = a.shape[:-3]
    n = len(lead)
    turned = a.reshape(lead + (2, 2, 16, 128)).transpose(
        tuple(range(n)) + (n, n + 2, n + 1, n + 3)
    )
    return turned.reshape(lead + (64, 128))


def from_rows(a):
    lead = a.shape[:-2]
    n = len(lead)
    turned = a.reshape(lead + (2, 16, 2, 128)).transpose(
        tuple(range(n)) + (n, n + 2, n + 1, n + 3)
    )
    return turned.reshape(lead + (2, 2, 2048))


def on_device(
    nx,
    ny,
    cell_offset,
    velocity,
    affine,
    cell_index,
    counts,
    cell_flags,
    old_pressure,
    destination,
    dest_slot,
):
    vmem = pl.BlockSpec(memory_space=pltpu.VMEM)
    anywhere = pl.BlockSpec(memory_space=pltpu.HBM)

    def f32(*shape):
        return pltpu.VMEM(shape, F32)

    def halos(count, reach):
        rows = [8 * reach, 8 * (reach + 1)] + [8 * corner_tiles(n, reach) for n in range(4, 8)]
        return [f32(count, n, 128) for n in rows]

    shapes = ((3, 64, 128), (3, 64, 128), (9, 64, 128), (8, 8, 128), (15, 16, 128))
    outs = pl.pallas_call(
        functools.partial(kernel, nx, ny),
        out_shape=[pltpu.VMEM(shape, F32) for shape in shapes],
        in_specs=[anywhere] * 9,
        out_specs=[vmem] * 5,
        scratch_shapes=[
            f32(3, 64, 128),
            f32(3, 64, 128),
            f32(9, 64, 128),
            pltpu.VMEM((64, 128), I32),
            pltpu.VMEM((2, 2, 32), I32),
            pltpu.VMEM((64, 128), I32),
            pltpu.VMEM((64, 128), I32),
            pltpu.VMEM((8, 8, 128), I32),
            f32(2, WIDE_X, 24, 128),
            f32(64, 128),
            pltpu.VMEM((64, 128), I32),
            f32(32 * 64, 128),
            f32(16, 32, 128),
            f32(10 * 10 * 16, 128),
            f32(4 * 9 * 8, 128),
            f32(4, 8, 128),
            f32(7, 8, 128),
            f32(5, 8, 128),
            f32(7, 8, 128),
            f32(5, 8, 128),
            f32(2, 8, 128),
            f32(1, 8, 128),
        ]
        + [f32(tiles, 8, 128) for tiles in SUM_TILES]
        + [
            halos(2, FIELD_REACH),
            halos(2, FIELD_REACH),
            halos(1, SOURCE_REACH),
            halos(1, SOURCE_REACH),
            f32(3, 10, 24, 128),
            f32(1, WIDE_X, 24, 128),
            f32(WIDE_X, 24, 128),
            f32(WIDE_X, 40, 128),
            f32(WIDE_X, 40, 128),
            f32(WIDE_X, 40, 128),
            f32(3, 9, 16, 128),
            f32(150 * 8, 128),
            pltpu.VMEM((256, 8192), BF16),
            pltpu.VMEM((256, 8192), BF16),
            f32(16 * 64, 128),
            f32(8, 16, 256),
            f32(8, 16, 256),
            pltpu.SemaphoreType.DMA((9,)),
            pltpu.SemaphoreType.DMA((32,)),
            pltpu.SemaphoreType.DMA((32,)),
        ],
        compiler_params=pltpu.CompilerParams(
            collective_id=0, has_side_effects=True, vmem_limit_bytes=60 * 1024 * 1024
        ),
        name="substep",
    )(
        *[
            pltpu.with_memory_space_constraint(a, pltpu.HBM)
            for a in (
                in_rows(cell_offset),
                in_rows(velocity),
                in_rows(affine),
                in_rows(cell_index),
                counts,
                cell_flags,
                old_pressure,
                in_rows(destination),
                in_rows(dest_slot),
            )
        ]
    )
    outs = pl.pallas_call(
        write_out,
        out_shape=[jax.ShapeDtypeStruct(shape, F32) for shape in shapes],
        in_specs=[vmem] * 5,
        out_specs=[anywhere] * 5,
        scratch_shapes=[pltpu.SemaphoreType.DMA((5,))],
        compiler_params=pltpu.CompilerParams(vmem_limit_bytes=60 * 1024 * 1024),
        name="write_out",
    )(*[pltpu.with_memory_space_constraint(a, pltpu.VMEM) for a in outs])
    return (
        from_rows(outs[0]),
        from_rows(outs[1]),
        from_rows(outs[2]),
        outs[3],
        outs[4].reshape(15, 8, 1, 256),
    )


def solution(mesh):
    particles, blocks = P(None, "gx", "gy", None), P("gx", "gy", None)
    return jax.shard_map(
        functools.partial(on_device, mesh.shape["gx"], mesh.shape["gy"]),
        mesh=mesh,
        in_specs=(particles, particles, particles) + (blocks,) * 6,
        out_specs=(particles, particles, particles, blocks, P(None, None, "gx", "gy")),
        check_vma=False,
    )
```

```python
import functools

import jax
import jax.numpy as jnp
from jax import lax
from jax.experimental import pallas as pl
from jax.experimental.pallas import tpu as pltpu
from jax.sharding import PartitionSpec as P

F32, BF16, I32 = jnp.float32, jnp.bfloat16, jnp.int32
MESH = pl.DeviceIdType.MESH
STEPS = ((1, 0), (-1, 0), (0, 1), (0, -1), (1, 1), (1, -1), (-1, 1), (-1, -1))
TIME_STEP = 0.25
GRAVITY = 1.0
MASS_FLOOR = 0.5
ITERS = 4

WIDE_X = 19
FIELD_REACH = ITERS + 1
SOURCE_REACH = ITERS


def corner_runs(number, reach):
    dx, dy = STEPS[number]
    runs = []
    for far in range(1, reach + 1) if dx > 0 else range(reach + 1):
        x = 8 - far if dx > 0 else far
        left = reach - far
        if dy > 0 and left > 0:
            runs.append((x, 8 - left, x - 8 * dx, -left, left))
        elif dy < 0:
            runs.append((x, 0, x - 8 * dx, 8, left + 1))
    return runs


def corner_tiles(number, reach):
    return -(-sum(run[4] for run in corner_runs(number, reach)) // 8)


SUM_TILES = (7, 5, 7, 5, 2, 1, 1, 1)


def iota(shape, dim):
    return lax.broadcasted_iota(I32, shape, dim)


def below_z(v):
    axis = v.ndim - 1
    return jnp.where(iota(v.shape, axis) == 0, 0.0, pltpu.roll(v, 1, axis))


def above_z(v):
    axis = v.ndim - 1
    return jnp.where(iota(v.shape, axis) == 127, 0.0, pltpu.roll(v, 127, axis))


def two_parts(v):
    high = v.astype(BF16)
    return high, (v - high.astype(F32)).astype(BF16)


def matches(row, count):
    places = iota((count, 128), 0).astype(F32).astype(BF16)
    wanted = jnp.broadcast_to(row.astype(F32), (count, 128)).astype(BF16)
    one, zero = jnp.ones((count, 128), BF16), jnp.zeros((count, 128), BF16)
    return jnp.where(places == wanted, one, zero)


def dot_last(a, b):
    return lax.dot_general(a, b, (((1,), (1,)), ((), ())), preferred_element_type=F32)


def blocks_exchanged(parts):
    parts = list(parts)
    group = iota(parts[0].shape, 1) >> 4
    for bit in (1, 2, 4):
        upper = (group & bit) != 0
        for i in range(8):
            if i & bit:
                continue
            low, high = parts[i], parts[i | bit]
            parts[i] = jnp.where(upper, pltpu.roll(high, 16 * bit, 1), low)
            parts[i | bit] = jnp.where(upper, high, pltpu.roll(low, 128 - 16 * bit, 1))
    return parts


def cell_row(x, y, ox, oy, k):
    return ((x + 1) * 10 + (y + 1)) * 16 + 8 * ox + 4 * oy + k


class Neighbourly:
    def __init__(self, copy, goes, comes):
        self.copy, self.goes, self.comes = copy, goes, comes

    def start(self):
        pl.when(self.goes)(self.copy.start)

    def wait_send(self):
        pl.when(self.goes)(self.copy.wait_send)

    def wait_recv(self):
        pl.when(self.comes)(self.copy.wait_recv)


def kernel(
    nx,
    ny,
    off_h,
    vel_h,
    aff_h,
    cell_h,
    count_h,
    flag_h,
    press_h,
    dest_h,
    slot_h,
    off_o,
    vel_o,
    aff_o,
    press_o,
    rec_o,
    off_v,
    vel_v,
    aff_v,
    cell_v,
    count_v,
    dest_v,
    slot_v,
    flag_v,
    field_w,
    alive_v,
    bin_v,
    quant,
    binned,
    cells,
    nodes,
    column8,
    message0,
    message1,
    message2,
    message3,
    message4,
    message_d2,
    arrive0,
    arrive1,
    arrive2,
    arrive3,
    arrive4,
    arrive5,
    arrive6,
    arrive7,
    field_out,
    field_in,
    source_out,
    source_in,
    speed_w,
    source_w,
    scale_w,
    solid_w,
    press_a,
    press_b,
    settled,
    tables,
    slot_onehot,
    parcels,
    records,
    outgoing,
    incoming,
    load_sem,
    send_sem,
    recv_sem,
):
    gx, gy = lax.axis_index("gx"), lax.axis_index("gy")
    where_x = {0: gx, 1: lax.rem(gx + 1, nx), -1: lax.rem(gx + nx - 1, nx)}
    where_y = {0: gy, 1: lax.rem(gy + 1, ny), -1: lax.rem(gy + ny - 1, ny)}
    inside_x = {0: gx >= 0, 1: gx < nx - 1, -1: gx > 0}
    inside_y = {0: gy >= 0, 1: gy < ny - 1, -1: gy > 0}

    def copy_to(number, stage, src, dst):
        dx, dy = STEPS[number]
        copy = pltpu.make_async_remote_copy(
            src_ref=src,
            dst_ref=dst,
            send_sem=send_sem.at[8 * stage + number],
            recv_sem=recv_sem.at[8 * stage + number],
            device_id=(where_x[dx], where_y[dy]),
            device_id_type=MESH,
        )
        goes = inside_x[dx] & inside_y[dy]
        comes = inside_x[-dx] & inside_y[-dy]
        return Neighbourly(copy, goes, comes)

    def flat_rows(field):
        return field.reshape(field.shape[0] * WIDE_X * 24, 128)

    def halo(stage, field, outs, ins, reach):
        flat = flat_rows(field)
        lows, highs = reach, reach + 1
        copies = [
            copy_to(
                0,
                stage,
                field.at[:, pl.ds(13 - lows, lows), pl.ds(8, 8)],
                field.at[:, pl.ds(5 - lows, lows), pl.ds(8, 8)],
            ),
            copy_to(
                1,
                stage,
                field.at[:, pl.ds(5, highs), pl.ds(8, 8)],
                field.at[:, pl.ds(13, highs), pl.ds(8, 8)],
            ),
        ]
        for number in range(2, 8):
            out = outs[number - 2]
            for c in range(field.shape[0]):
                if number < 4:
                    first, columns = (8 - lows, lows) if number == 2 else (0, highs)
                    for j in range(columns):
                        start = (c * WIDE_X + 5) * 24 + 8 + first + j
                        out[c, pl.ds(8 * j, 8)] = flat[pl.ds(start, 8, stride=24), :]
                else:
                    row = 0
                    for x, y, _, _, length in corner_runs(number, reach):
                        out[c, row : row + length] = field[c, x + 5, y + 8 : y + 8 + length]
                        row += length
            copies.append(copy_to(number, stage, out, ins[number - 2]))
        return copies

    def unpack(field, ins, reach):
        flat = flat_rows(field)
        for number in range(2, 8):
            got = ins[number - 2]
            for c in range(field.shape[0]):
                if number < 4:
                    first, columns = (8 - reach, reach) if number == 2 else (16, reach + 1)
                    for j in range(columns):
                        start = (c * WIDE_X + 5) * 24 + first + j
                        flat[pl.ds(start, 8, stride=24), :] = got[c, pl.ds(8 * j, 8)]
                else:
                    row = 0
                    for _, _, x, y, length in corner_runs(number, reach):
                        field[c, x + 5, y + 8 : y + 8 + length] = got[c, row : row + length]
                        row += length

    def kept(v, dx, dy):
        if dx:
            v = jnp.where(inside_x[dx], v, 0.0)
        if dy:
            v = jnp.where(inside_y[dy], v, 0.0)
        return v

    own = (1, pl.ds(5, 8), pl.ds(8, 8))
    loads = [
        pltpu.make_async_copy(src, dst, load_sem.at[i])
        for i, (src, dst) in enumerate(
            (
                (flag_h, flag_v),
                (press_h, field_w.at[own]),
                (count_h, count_v),
                (cell_h, cell_v),
                (off_h, off_v),
                (vel_h, vel_v),
                (aff_h, aff_v),
                (slot_h, slot_v),
                (dest_h, dest_v),
            )
        )
    ]
    for load in loads:
        load.start()

    barrier = pltpu.get_barrier_semaphore()
    for dx, dy in STEPS:
        pl.when(inside_x[dx] & inside_y[dy])(
            functools.partial(
                pl.semaphore_signal,
                barrier,
                inc=1,
                device_id=(where_x[dx], where_y[dy]),
                device_id_type=MESH,
            )
        )
    near_x = 1 + inside_x[1].astype(I32) + inside_x[-1].astype(I32)
    near_y = 1 + inside_y[1].astype(I32) + inside_y[-1].astype(I32)

    zero_tile = jnp.zeros((8, 128), F32)
    for x in range(WIDE_X):
        for field in (solid_w, press_a, press_b):
            field[x, 0:8] = zero_tile
            field[x, 32:40] = zero_tile
    for x in range(8):
        for half in (0, 8):
            cells[pl.ds(cell_row(x, -1, 0, 0, 0) + half, 8), :] = zero_tile
    for half in (0, 8):
        cells[pl.ds(cell_row(-1, 7, 0, 0, 0) + half, 8), :] = zero_tile

    pl.semaphore_wait(barrier, near_x * near_y - 1)
    loads[0].wait()
    loads[1].wait()

    for x in range(8):
        field_w[0, x + 5, 8:16] = flag_v[x].astype(F32)
    exchanges = halo(0, field_w, field_out, field_in, FIELD_REACH)
    for copy in exchanges:
        copy.start()

    for load in loads[2:7]:
        load.wait()

    sub32 = iota((32, 128), 0)
    lane32 = iota((32, 128), 1)
    for xb in range(2):
        r0 = 32 * xb
        row = iota((32, 32), 0)
        column = iota((32, 32), 1)
        totals = count_v[xb].astype(F32)
        spread = jnp.where(
            (row & 1) == 0,
            jnp.broadcast_to(totals[0:1], (32, 32)),
            jnp.broadcast_to(totals[1:2], (32, 32)),
        )
        spread = jnp.where((column >> 1) == (row >> 1), spread, 0.0).astype(BF16)
        half = ((sub32 & 1) == (lane32 >> 6)).astype(F32).astype(BF16)
        live = jnp.dot(spread, half, preferred_element_type=F32)
        alive_v[pl.ds(r0, 32), :] = jnp.where(
            (lane32 & 63).astype(F32) < live, 1.0, 0.0
        )
        number_in_block = cell_v[pl.ds(r0, 32), :]
        bin_v[pl.ds(r0, 32), :] = (
            ((number_in_block >> 2) << 4)
            + (((sub32 >> 1) & 1) << 3)
            + ((lane32 >> 6) << 2)
            + (number_in_block & 3)
        )

    def deposit(step, carry):
        rows = pl.ds(pl.multiple_of(step * 16, 16), 16)
        alive = alive_v[rows, :]
        f = [off_v[d, rows, :] for d in range(3)]
        a = [aff_v[j, rows, :] for j in range(9)]
        base = [
            vel_v[k, rows, :] - (a[3 * k] * f[0] + a[3 * k + 1] * f[1] + a[3 * k + 2] * f[2])
            for k in range(3)
        ]
        hx = [(1.0 - f[0]) * alive, f[0] * alive]
        hy = [1.0 - f[1], f[1]]
        hz = [1.0 - f[2], f[2]]
        for ox in range(2):
            bx = [base[k] + a[3 * k] if ox else base[k] for k in range(3)]
            for oy in range(2):
                by = [bx[k] + a[3 * k + 1] if oy else bx[k] for k in range(3)]
                hxy = hx[ox] * hy[oy]
                for oz in range(2):
                    w = hxy * hz[oz]
                    channel = 16 * oz + 8 * ox + 4 * oy
                    start = pl.multiple_of(channel * 64 + step * 16, 16)
                    quant[pl.ds(start, 16), :] = w
                    for k in range(3):
                        bz = by[k] + a[3 * k + 2] if oz else by[k]
                        start = pl.multiple_of((channel + k + 1) * 64 + step * 16, 16)
                        quant[pl.ds(start, 16), :] = w * bz
        return carry

    lax.fori_loop(0, 4, deposit, 0)

    def bin_column(col, carry):
        xb, yb = col // 2, lax.rem(col, 2)
        first_z = (iota((16, 128), 1) & 15) == 0
        before = [0.0, 0.0]
        for pair in range(8):
            sides, hots = [], []
            for j in range(2):
                r = 32 * xb + yb + 4 * pair + 2 * j
                high, low = two_parts(quant[pl.ds(r, 32, stride=64), :])
                sides.append(jnp.concatenate([high, low], axis=0))
                hots.append(matches(bin_v[pl.ds(r, 1), :], 256))
            total = dot_last(jnp.concatenate(sides, axis=1), jnp.concatenate(hots, axis=1))
            total = total[0:32] + total[32:64]
            for h in range(2):
                lower = total[0:16, 128 * h : 128 * h + 128]
                upper = total[16:32, 128 * h : 128 * h + 128]
                carried = before[h]
                before[h] = pltpu.roll(upper, 113, 1)
                binned[2 * pair + h] = lower + jnp.where(
                    first_z, carried, pltpu.roll(upper, 1, 1)
                )
        for h in range(2):
            for g in range(2):
                parts = blocks_exchanged(
                    [binned[2 * pair + h, 8 * g : 8 * g + 8] for pair in range(8)]
                )
                for i in range(8):
                    q = 8 * h + i
                    start = ((4 * xb + q // 4 + 1) * 10 + 4 * yb + q % 4 + 1) * 16 + 8 * g
                    cells[pl.ds(pl.multiple_of(start, 8), 8), :] = parts[i]
        return carry

    lax.fori_loop(0, 4, bin_column, 0, unroll=4)

    for k in range(4):
        for x in range(9):
            total = None
            for ox in range(2):
                if not 0 <= x - ox < 8:
                    continue
                for oy in range(2):
                    part = cells[pl.ds(cell_row(x - ox, -oy, ox, oy, k), 8, stride=16), :]
                    total = part if total is None else total + part
            nodes[pl.ds((k * 9 + x) * 8, 8), :] = total
        column8[k] = (
            cells[pl.ds(cell_row(0, 7, 0, 1, k), 8, stride=160), :]
            + cells[pl.ds(cell_row(-1, 7, 1, 1, k), 8, stride=160), :]
        )

    def four(x, y, ox, oy):
        return cells[pl.ds(cell_row(x, y, ox, oy, 0), 4), :]

    corner88 = four(7, 7, 1, 1)
    d1 = jnp.concatenate([corner88, four(0, 7, 0, 1)], axis=0)
    d2 = jnp.concatenate([four(7, 0, 1, 0), four(0, 0, 0, 0)], axis=0)
    d3 = jnp.concatenate(
        [four(7, 7, 0, 1) + four(6, 7, 1, 1), four(7, 7, 1, 0) + four(7, 6, 1, 1)], axis=0
    )
    for k in range(4):
        message0[k] = nodes[pl.ds((k * 9 + 8) * 8, 8), :]
        message1[k] = nodes[pl.ds(k * 72, 8), :]
        message2[k] = column8[k]
        message3[k] = nodes[pl.ds(k * 72, 8, stride=8), :]
    for i, k in enumerate((0, 1)):
        message0[4 + i] = nodes[pl.ds((k * 9 + 7) * 8, 8), :]
    for i, k in enumerate((0, 2)):
        message2[4 + i] = nodes[pl.ds(k * 72 + 7, 8, stride=8), :]
    message0[6] = d1
    message1[4] = d1
    message2[6] = d1
    message3[4] = d2
    message4[0] = d1
    message4[1] = d3
    message_d2[0] = d2

    sums = [
        copy_to(number, 1, src, dst)
        for number, src, dst in (
            (0, message0, arrive0),
            (1, message1, arrive1),
            (2, message2, arrive2),
            (3, message3, arrive3),
            (4, message4, arrive4),
            (5, message_d2, arrive5),
            (6, message4.at[pl.ds(0, 1)], arrive6),
            (7, message_d2, arrive7),
        )
    ]
    for copy in sums:
        copy.start()

    loads[7].wait()
    loads[8].wait()

    def slot_rows(step, carry):
        for j in range(4):
            r = 4 * step + j
            slot = jnp.where(dest_v[pl.ds(r, 1), :] > 0, slot_v[pl.ds(r, 1), :], -1)
            lanes = pl.ds(pl.multiple_of(r * 128, 128), 128)
            slot_onehot[:, lanes] = matches(slot, 256)
        return carry

    for copy in exchanges:
        copy.wait_recv()
    unpack(field_w, field_in, FIELD_REACH)

    sub24 = iota((24, 128), 0)
    ok_y = (
        jnp.where(sub24 < 8, inside_y[-1].astype(I32), 1)
        * jnp.where(sub24 >= 16, inside_y[1].astype(I32), 1)
    ) > 0
    for x in range(WIDE_X):
        side = -1 if x < 5 else 1 if x >= 13 else 0
        kind = kept(jnp.where(ok_y, field_w[0, x], 0.0), side, 0)
        solid_w[x, 8:32] = jnp.where(kind == 2.0, 1.0, 0.0)
        fluid = kind == 1.0
        scale_w[x] = jnp.where(fluid, 1.0, 0.0)
        press_a[x, 8:32] = jnp.where(fluid, field_w[1, x], 0.0)
    for x in range(1, WIDE_X - 1):
        middle = solid_w[x, 8:32]
        closed = (
            solid_w[x - 1, 8:32]
            + solid_w[x + 1, 8:32]
            + solid_w[x, 7:31]
            + solid_w[x, 9:33]
            + below_z(middle)
            + above_z(middle)
        )
        scale_w[x] = scale_w[x] / jnp.maximum(6.0 - closed, 1.0)

    lax.fori_loop(0, 8, slot_rows, 0)

    for copy in sums:
        copy.wait_recv()

    sub8 = iota((8, 128), 0)

    def at_first(v, row):
        return jnp.where(sub8 == 0, v + row, v)

    speed_f = speed_w.reshape(3 * 10 * 24, 128)
    field_f = flat_rows(field_w)

    def normalised(sums4, kind, dx, dy, components=(0, 1, 2)):
        inverse = 1.0 / jnp.maximum(sums4[0], MASS_FLOOR)
        result = []
        for k in components:
            u = sums4[k + 1] * inverse
            if k == 2:
                u = u - TIME_STEP * GRAVITY
            result.append(kept(jnp.where(kind == 2.0, 0.0, u), dx, dy))
        return result

    minus_rows, below_columns = [None] * 4, [None] * 4
    for i, k in enumerate((0, 1)):
        minus_rows[k] = at_first(
            kept(arrive0[4 + i], -1, 0), kept(arrive4[1, k : k + 1], -1, -1)
        )
    for i, k in enumerate((0, 2)):
        below_columns[k] = at_first(
            kept(arrive2[4 + i], 0, -1), kept(arrive4[1, 4 + k : 5 + k], -1, -1)
        )
    plus_rows, upper_columns = [], []
    for k in range(4):
        first = nodes[pl.ds(k * 72, 8), :] + kept(arrive0[k], -1, 0)
        nodes[pl.ds(k * 72, 8), :] = first
        column = at_first(
            kept(arrive2[k], 0, -1), kept(arrive4[0, k : k + 1], -1, -1)
        )
        nodes[pl.ds(k * 72, 8, stride=8), :] = (
            nodes[pl.ds(k * 72, 8, stride=8), :] + column
        )
        plus_rows.append(
            at_first(
                nodes[pl.ds((k * 9 + 8) * 8, 8), :] + kept(arrive1[k], 1, 0),
                kept(arrive2[6, k : k + 1], 0, -1)
                + kept(arrive6[0, 4 + k : 5 + k], 1, -1),
            )
        )
        upper_columns.append(
            at_first(
                column8[k] + kept(arrive3[k], 0, 1),
                kept(arrive0[6, k : k + 1], -1, 0) + kept(arrive5[0, k : k + 1], -1, 1),
            )
        )
    corner = (
        message4[0, 0:4]
        + kept(arrive1[4, 4:8], 1, 0)
        + kept(arrive3[4, 0:4], 0, 1)
        + kept(arrive7[0, 4:8], 1, 1)
    )

    for x in range(-1, 9):
        if x == -1:
            sums4, side = minus_rows, -1
        elif x == 8:
            sums4, side = plus_rows, 1
        else:
            sums4 = [nodes[pl.ds((k * 9 + x) * 8, 8), :] for k in range(4)]
            side = 0
        wanted = (0,) if x == -1 else (0, 1, 2)
        u = normalised(sums4, field_w[0, x + 5, 8:16], side, 0, wanted)
        for k in wanted:
            speed_w[k, x + 1, 8:16] = u[k]
    for columns, y, side, wanted in (
        (below_columns, 7, -1, (1,)),
        (upper_columns, 16, 1, (0, 1, 2)),
    ):
        kind = field_f[pl.ds(5 * 24 + y, 8, stride=24), :]
        u = normalised(columns, kind, 0, side, wanted)
        for i, k in enumerate(wanted):
            speed_f[pl.ds((k * 10 + 1) * 24 + y, 8, stride=24), :] = u[i]
    u = normalised([corner[k : k + 1] for k in range(4)], field_w[0, 13, 16:17], 1, 1)
    for k in range(3):
        speed_w[k, 9, 16:17] = u[k]

    for x in range(8):
        source_w[0, x + 5, 8:16] = 0.5 * (
            speed_w[0, x + 2, 8:16]
            - speed_w[0, x, 8:16]
            + (speed_w[1, x + 1, 9:17] - speed_w[1, x + 1, 7:15])
            + (above_z(speed_w[2, x + 1, 8:16]) - below_z(speed_w[2, x + 1, 8:16]))
        )

    margins = halo(2, source_w, source_out, source_in, SOURCE_REACH)
    for copy in margins:
        copy.start()
    lax.fori_loop(8, 16, slot_rows, 0)
    for copy in margins:
        copy.wait_recv()
    unpack(source_w, source_in, SOURCE_REACH)

    old, new = press_a, press_b
    for sweep in range(ITERS):
        low, high = sweep + 1, WIDE_X - 1 - sweep
        for x in range(low, high):
            middle = old[x, 8:32]
            near = (
                old[x - 1, 8:32]
                + old[x + 1, 8:32]
                + old[x, 7:31]
                + old[x, 9:33]
                + below_z(middle)
                + above_z(middle)
            )
            scale = scale_w[x]
            new[x, 8:32] = jnp.where(scale > 0.0, scale * (near - source_w[0, x]), 0.0)
        old, new = new, old
    for x in range(8):
        press_o[x] = old[x + 5, 16:24]

    for x in range(9):
        w = x + 5
        p, s = old[w, 16:32], solid_w[w, 16:32]
        fluid = scale_w[w, 8:24] > 0.0
        slopes = (
            old[w + 1, 16:32]
            - old[w - 1, 16:32]
            + p * (solid_w[w + 1, 16:32] - solid_w[w - 1, 16:32]),
            old[w, 17:33]
            - old[w, 15:31]
            + p * (solid_w[w, 17:33] - solid_w[w, 15:31]),
            above_z(p) - below_z(p) + p * (above_z(s) - below_z(s)),
        )
        for k in range(3):
            settled[k, x] = speed_w[k, x + 1, 8:24] - jnp.where(fluid, 0.5 * slopes[k], 0.0)

    odd8 = (iota((8, 128), 0) & 1) == 1
    sub8 = iota((8, 128), 0)
    lane8 = iota((8, 128), 1)

    def table_row(k, ix, iy, j):
        return pl.ds(8 * (((k * 5 + ix) * 5 + iy) * 2 + j), 8)

    def sample_blocks(xb, carry):
        for k in range(3):
            for ix in range(5):
                for iy in range(5):
                    even = jnp.broadcast_to(settled[k, 4 * xb + ix, iy : iy + 1], (8, 128))
                    odd = jnp.broadcast_to(settled[k, 4 * xb + ix, iy + 4 : iy + 5], (8, 128))
                    table = jnp.where(odd8, odd, even)
                    tables[table_row(k, ix, iy, 0), :] = table
                    tables[table_row(k, ix, iy, 1), :] = above_z(table) - table
        return lax.fori_loop(0, 4, functools.partial(sample_rows, xb), carry, unroll=4)

    def sample_rows(xb, g, carry):
        start = pl.multiple_of(32 * xb + 8 * g, 8)
        rows = pl.ds(start, 8)
        cell = cell_v[rows, :]
        alive = alive_v[rows, :]
        qx, qy = cell >> 4, (cell >> 2) & 3
        z = ((4 * g + (sub8 >> 1)) << 3) + ((lane8 >> 6) << 2) + (cell & 3)
        at_x = [qx == i for i in range(4)]
        at_y = [qy == i for i in range(4)]
        f = [off_v[d, rows, :] for d in range(3)]

        def record_row(number):
            return pl.ds(pl.multiple_of(number * 64 + start, 8), 8)

        moving = dest_v[rows, :]

        def one_of(*numbers):
            hit = moving == numbers[0]
            for number in numbers[1:]:
                hit = hit | (moving == number)
            return jnp.where(hit, 8, 0)

        place = (
            4 * xb + qx - one_of(1, 5, 6) + one_of(2, 7, 8),
            ((sub8 & 1) << 2) + qy - one_of(3, 5, 7) + one_of(4, 6, 8),
            z,
        )
        for k in range(3):
            pick_x = [[None] * 4, [None] * 4]
            for ix in range(5):
                pick_y = [[None] * 2, [None] * 2]
                for iy in range(5):
                    got = [
                        jnp.take_along_axis(tables[table_row(k, ix, iy, j), :], z, axis=1)
                        for j in range(2)
                    ]
                    for o in range(2):
                        if not 0 <= iy - o < 4:
                            continue
                        for j in range(2):
                            held = pick_y[o][j]
                            pick_y[o][j] = (
                                got[j]
                                if held is None
                                else jnp.where(at_y[iy - o], got[j], held)
                            )
                flat = pick_y[0] + pick_y[1]
                for o in range(2):
                    if not 0 <= ix - o < 4:
                        continue
                    for j in range(4):
                        held = pick_x[o][j]
                        pick_x[o][j] = (
                            flat[j] if held is None else jnp.where(at_x[ix - o], flat[j], held)
                        )
            value, along_y, along_z = [], [], []
            for o in range(2):
                a0, rise0, a1, rise1 = pick_x[o]
                v0 = a0 + f[2] * rise0
                v1 = a1 + f[2] * rise1
                along_y.append(v1 - v0)
                value.append(v0 + f[1] * (v1 - v0))
                along_z.append(rise0 + f[1] * (rise1 - rise0))
            along_x = value[1] - value[0]
            speed = (value[0] + f[0] * along_x) * alive
            offset = f[k] + TIME_STEP * speed
            slope = (
                along_x * alive,
                (along_y[0] + f[0] * (along_y[1] - along_y[0])) * alive,
                (along_z[0] + f[0] * (along_z[1] - along_z[0])) * alive,
            )
            off_o[k, rows, :] = offset
            vel_o[k, rows, :] = speed
            records[record_row(k), :] = place[k].astype(F32) + offset
            records[record_row(3 + k), :] = speed
            for b in range(3):
                aff_o[3 * k + b, rows, :] = slope[b]
                records[record_row(6 + 3 * k + b), :] = slope[b]
        records[record_row(15), :] = jnp.zeros((8, 128), F32)
        for j in range(8):
            r = start + j
            record = records[pl.ds(r, 16, stride=64), :]
            high, low = two_parts(record)
            both = jnp.concatenate([high, low], axis=0)
            moving = jnp.broadcast_to(dest_v[pl.ds(r, 1), :].astype(F32), (32, 128)).astype(BF16)
            lanes = pl.ds(pl.multiple_of(r * 128, 128), 128)
            for number in range(8):
                hit = moving == jnp.full((32, 128), number + 1, BF16)
                parcels[pl.ds(32 * number, 32), lanes] = jnp.where(hit, both, jnp.zeros_like(both))
        return carry

    lax.fori_loop(0, 2, sample_blocks, 0)


    placed = dot_last(parcels[...], slot_onehot[...])
    leaving = [None] * 8
    for number in (4, 5, 6, 7, 0, 1, 2, 3):
        first = 32 * number
        outgoing[number] = placed[first : first + 16] + placed[first + 16 : first + 32]
        leaving[number] = copy_to(number, 3, outgoing.at[number], incoming.at[number])
        leaving[number].start()

    for copy in exchanges + sums + margins:
        copy.wait_send()

    rec_f = rec_o.reshape(15 * 16, 128)
    for number in (4, 5, 6, 7, 0, 1, 2, 3):
        leaving[number].wait_recv()
        leaving[number].wait_send()
        dx, dy = STEPS[number]
        arrived = kept(incoming[number], -dx, -dy)
        for half in range(2):
            rec_f[pl.ds(2 * number + half, 15, stride=16), :] = arrived[
                0:15, 128 * half : 128 * half + 128
            ]


def write_out(*refs):
    copies = [
        pltpu.make_async_copy(refs[i], refs[5 + i], refs[10].at[i]) for i in range(5)
    ]
    for copy in copies:
        copy.start()
    for copy in copies:
        copy.wait()


def in_rows(a):
    lead = a.shape[:-3]
    n = len(lead)
    turned = a.reshape(lead + (2, 2, 16, 128)).transpose(
        tuple(range(n)) + (n, n + 2, n + 1, n + 3)
    )
    return turned.reshape(lead + (64, 128))


def from_rows(a):
    lead = a.shape[:-2]
    n = len(lead)
    turned = a.reshape(lead + (2, 16, 2, 128)).transpose(
        tuple(range(n)) + (n, n + 2, n + 1, n + 3)
    )
    return turned.reshape(lead + (2, 2, 2048))


def on_device(
    nx,
    ny,
    cell_offset,
    velocity,
    affine,
    cell_index,
    counts,
    cell_flags,
    old_pressure,
    destination,
    dest_slot,
):
    vmem = pl.BlockSpec(memory_space=pltpu.VMEM)
    anywhere = pl.BlockSpec(memory_space=pltpu.HBM)

    def f32(*shape):
        return pltpu.VMEM(shape, F32)

    def halos(count, reach):
        rows = [8 * reach, 8 * (reach + 1)] + [8 * corner_tiles(n, reach) for n in range(4, 8)]
        return [f32(count, n, 128) for n in rows]

    shapes = ((3, 64, 128), (3, 64, 128), (9, 64, 128), (8, 8, 128), (15, 16, 128))
    outs = pl.pallas_call(
        functools.partial(kernel, nx, ny),
        out_shape=[pltpu.VMEM(shape, F32) for shape in shapes],
        in_specs=[anywhere] * 9,
        out_specs=[vmem] * 5,
        scratch_shapes=[
            f32(3, 64, 128),
            f32(3, 64, 128),
            f32(9, 64, 128),
            pltpu.VMEM((64, 128), I32),
            pltpu.VMEM((2, 2, 32), I32),
            pltpu.VMEM((64, 128), I32),
            pltpu.VMEM((64, 128), I32),
            pltpu.VMEM((8, 8, 128), I32),
            f32(2, WIDE_X, 24, 128),
            f32(64, 128),
            pltpu.VMEM((64, 128), I32),
            f32(32 * 64, 128),
            f32(16, 16, 128),
            f32(10 * 10 * 16, 128),
            f32(4 * 9 * 8, 128),
            f32(4, 8, 128),
            f32(7, 8, 128),
            f32(5, 8, 128),
            f32(7, 8, 128),
            f32(5, 8, 128),
            f32(2, 8, 128),
            f32(1, 8, 128),
        ]
        + [f32(tiles, 8, 128) for tiles in SUM_TILES]
        + [
            halos(2, FIELD_REACH),
            halos(2, FIELD_REACH),
            halos(1, SOURCE_REACH),
            halos(1, SOURCE_REACH),
            f32(3, 10, 24, 128),
            f32(1, WIDE_X, 24, 128),
            f32(WIDE_X, 24, 128),
            f32(WIDE_X, 40, 128),
            f32(WIDE_X, 40, 128),
            f32(WIDE_X, 40, 128),
            f32(3, 9, 16, 128),
            f32(150 * 8, 128),
            pltpu.VMEM((256, 8192), BF16),
            pltpu.VMEM((256, 8192), BF16),
            f32(16 * 64, 128),
            f32(8, 16, 256),
            f32(8, 16, 256),
            pltpu.SemaphoreType.DMA((9,)),
            pltpu.SemaphoreType.DMA((32,)),
            pltpu.SemaphoreType.DMA((32,)),
        ],
        compiler_params=pltpu.CompilerParams(
            collective_id=0, has_side_effects=True, vmem_limit_bytes=60 * 1024 * 1024
        ),
        name="substep",
    )(
        *[
            pltpu.with_memory_space_constraint(a, pltpu.HBM)
            for a in (
                in_rows(cell_offset),
                in_rows(velocity),
                in_rows(affine),
                in_rows(cell_index),
                counts,
                cell_flags,
                old_pressure,
                in_rows(destination),
                in_rows(dest_slot),
            )
        ]
    )
    outs = pl.pallas_call(
        write_out,
        out_shape=[jax.ShapeDtypeStruct(shape, F32) for shape in shapes],
        in_specs=[vmem] * 5,
        out_specs=[anywhere] * 5,
        scratch_shapes=[pltpu.SemaphoreType.DMA((5,))],
        compiler_params=pltpu.CompilerParams(vmem_limit_bytes=60 * 1024 * 1024),
        name="write_out",
    )(*[pltpu.with_memory_space_constraint(a, pltpu.VMEM) for a in outs])
    return (
        from_rows(outs[0]),
        from_rows(outs[1]),
        from_rows(outs[2]),
        outs[3],
        outs[4].reshape(15, 8, 1, 256),
    )


def solution(mesh):
    particles, blocks = P(None, "gx", "gy", None), P("gx", "gy", None)
    return jax.shard_map(
        functools.partial(on_device, mesh.shape["gx"], mesh.shape["gy"]),
        mesh=mesh,
        in_specs=(particles, particles, particles) + (blocks,) * 6,
        out_specs=(particles, particles, particles, blocks, P(None, None, "gx", "gy")),
        check_vma=False,
    )
```

```python
import functools

import jax
import jax.numpy as jnp
from jax import lax
from jax.experimental import pallas as pl
from jax.experimental.pallas import tpu as pltpu
from jax.sharding import PartitionSpec as P

F32, BF16, I32 = jnp.float32, jnp.bfloat16, jnp.int32
MESH = pl.DeviceIdType.MESH
STEPS = ((1, 0), (-1, 0), (0, 1), (0, -1), (1, 1), (1, -1), (-1, 1), (-1, -1))
TIME_STEP = 0.25
GRAVITY = 1.0
MASS_FLOOR = 0.5
ITERS = 4

WIDE_X = 19
FIELD_REACH = ITERS + 1
SOURCE_REACH = ITERS


def corner_runs(number, reach):
    dx, dy = STEPS[number]
    runs = []
    for far in range(1, reach + 1) if dx > 0 else range(reach + 1):
        x = 8 - far if dx > 0 else far
        left = reach - far
        if dy > 0 and left > 0:
            runs.append((x, 8 - left, x - 8 * dx, -left, left))
        elif dy < 0:
            runs.append((x, 0, x - 8 * dx, 8, left + 1))
    return runs


def corner_tiles(number, reach):
    return -(-sum(run[4] for run in corner_runs(number, reach)) // 8)


SUM_TILES = (8, 6, 8, 6, 2, 1, 1, 2)


def iota(shape, dim):
    return lax.broadcasted_iota(I32, shape, dim)


def below_z(v):
    axis = v.ndim - 1
    return jnp.where(iota(v.shape, axis) == 0, 0.0, pltpu.roll(v, 1, axis))


def above_z(v):
    axis = v.ndim - 1
    return jnp.where(iota(v.shape, axis) == 127, 0.0, pltpu.roll(v, 127, axis))


def two_parts(v):
    high = v.astype(BF16)
    return high, (v - high.astype(F32)).astype(BF16)


def matches(row, count):
    places = iota((count, 128), 0).astype(F32).astype(BF16)
    wanted = jnp.broadcast_to(row.astype(F32), (count, 128)).astype(BF16)
    one, zero = jnp.ones((count, 128), BF16), jnp.zeros((count, 128), BF16)
    return jnp.where(places == wanted, one, zero)


def dot_last(a, b):
    return lax.dot_general(a, b, (((1,), (1,)), ((), ())), preferred_element_type=F32)


def blocks_exchanged(parts):
    parts = list(parts)
    group = iota(parts[0].shape, 1) >> 4
    for bit in (1, 2, 4):
        upper = (group & bit) != 0
        for i in range(8):
            if i & bit:
                continue
            low, high = parts[i], parts[i | bit]
            parts[i] = jnp.where(upper, pltpu.roll(high, 16 * bit, 1), low)
            parts[i | bit] = jnp.where(upper, high, pltpu.roll(low, 128 - 16 * bit, 1))
    return parts


def cell_row(x, y, ox, oy, k):
    return ((x + 1) * 10 + (y + 1)) * 16 + 8 * ox + 4 * oy + k


class Neighbourly:
    def __init__(self, copy, goes, comes):
        self.copy, self.goes, self.comes = copy, goes, comes

    def start(self):
        pl.when(self.goes)(self.copy.start)

    def wait_send(self):
        pl.when(self.goes)(self.copy.wait_send)

    def wait_recv(self):
        pl.when(self.comes)(self.copy.wait_recv)


def kernel(
    nx,
    ny,
    off_h,
    vel_h,
    aff_h,
    cell_h,
    count_h,
    flag_h,
    press_h,
    dest_h,
    slot_h,
    off_o,
    vel_o,
    aff_o,
    press_o,
    rec_o,
    off_v,
    vel_v,
    aff_v,
    cell_v,
    count_v,
    dest_v,
    slot_v,
    flag_v,
    field_w,
    alive_v,
    bin_v,
    quant,
    binned,
    cells,
    nodes,
    column8,
    message0,
    message1,
    message2,
    message3,
    message4,
    message7,
    arrive0,
    arrive1,
    arrive2,
    arrive3,
    arrive4,
    arrive5,
    arrive6,
    arrive7,
    field_out,
    field_in,
    source_out,
    source_in,
    speed_w,
    source_w,
    scale_w,
    solid_w,
    press_a,
    press_b,
    settled,
    tables,
    slot_onehot,
    parcels,
    records,
    outgoing,
    incoming,
    load_sem,
    send_sem,
    recv_sem,
):
    gx, gy = lax.axis_index("gx"), lax.axis_index("gy")
    where_x = {0: gx, 1: lax.rem(gx + 1, nx), -1: lax.rem(gx + nx - 1, nx)}
    where_y = {0: gy, 1: lax.rem(gy + 1, ny), -1: lax.rem(gy + ny - 1, ny)}
    inside_x = {0: gx >= 0, 1: gx < nx - 1, -1: gx > 0}
    inside_y = {0: gy >= 0, 1: gy < ny - 1, -1: gy > 0}

    def copy_to(number, stage, src, dst):
        dx, dy = STEPS[number]
        copy = pltpu.make_async_remote_copy(
            src_ref=src,
            dst_ref=dst,
            send_sem=send_sem.at[8 * stage + number],
            recv_sem=recv_sem.at[8 * stage + number],
            device_id=(where_x[dx], where_y[dy]),
            device_id_type=MESH,
        )
        goes = inside_x[dx] & inside_y[dy]
        comes = inside_x[-dx] & inside_y[-dy]
        return Neighbourly(copy, goes, comes)

    def flat_rows(field):
        return field.reshape(field.shape[0] * WIDE_X * 24, 128)

    def halo(stage, field, outs, ins, reach):
        flat = flat_rows(field)
        lows, highs = reach, reach + 1
        copies = [
            copy_to(
                0,
                stage,
                field.at[:, pl.ds(13 - lows, lows), pl.ds(8, 8)],
                field.at[:, pl.ds(5 - lows, lows), pl.ds(8, 8)],
            ),
            copy_to(
                1,
                stage,
                field.at[:, pl.ds(5, highs), pl.ds(8, 8)],
                field.at[:, pl.ds(13, highs), pl.ds(8, 8)],
            ),
        ]
        for number in range(2, 8):
            out = outs[number - 2]
            for c in range(field.shape[0]):
                if number < 4:
                    first, columns = (8 - lows, lows) if number == 2 else (0, highs)
                    for j in range(columns):
                        start = (c * WIDE_X + 5) * 24 + 8 + first + j
                        out[c, pl.ds(8 * j, 8)] = flat[pl.ds(start, 8, stride=24), :]
                else:
                    row = 0
                    for x, y, _, _, length in corner_runs(number, reach):
                        out[c, row : row + length] = field[c, x + 5, y + 8 : y + 8 + length]
                        row += length
            copies.append(copy_to(number, stage, out, ins[number - 2]))
        return copies

    def unpack(field, ins, reach):
        flat = flat_rows(field)
        for number in range(2, 8):
            got = ins[number - 2]
            for c in range(field.shape[0]):
                if number < 4:
                    first, columns = (8 - reach, reach) if number == 2 else (16, reach + 1)
                    for j in range(columns):
                        start = (c * WIDE_X + 5) * 24 + first + j
                        flat[pl.ds(start, 8, stride=24), :] = got[c, pl.ds(8 * j, 8)]
                else:
                    row = 0
                    for _, _, x, y, length in corner_runs(number, reach):
                        field[c, x + 5, y + 8 : y + 8 + length] = got[c, row : row + length]
                        row += length

    def kept(v, dx, dy):
        if dx:
            v = jnp.where(inside_x[dx], v, 0.0)
        if dy:
            v = jnp.where(inside_y[dy], v, 0.0)
        return v

    own = (1, pl.ds(5, 8), pl.ds(8, 8))
    loads = [
        pltpu.make_async_copy(src, dst, load_sem.at[i])
        for i, (src, dst) in enumerate(
            (
                (flag_h, flag_v),
                (press_h, field_w.at[own]),
                (count_h, count_v),
                (cell_h, cell_v),
                (off_h, off_v),
                (vel_h, vel_v),
                (aff_h, aff_v),
                (slot_h, slot_v),
                (dest_h, dest_v),
            )
        )
    ]
    for load in loads:
        load.start()

    barrier = pltpu.get_barrier_semaphore()
    for dx, dy in STEPS:
        pl.when(inside_x[dx] & inside_y[dy])(
            functools.partial(
                pl.semaphore_signal,
                barrier,
                inc=1,
                device_id=(where_x[dx], where_y[dy]),
                device_id_type=MESH,
            )
        )
    near_x = 1 + inside_x[1].astype(I32) + inside_x[-1].astype(I32)
    near_y = 1 + inside_y[1].astype(I32) + inside_y[-1].astype(I32)

    zero_tile = jnp.zeros((8, 128), F32)
    for x in range(WIDE_X):
        for field in (solid_w, press_a, press_b):
            field[x, 0:8] = zero_tile
            field[x, 32:40] = zero_tile
    for x in range(8):
        for half in (0, 8):
            cells[pl.ds(cell_row(x, -1, 0, 0, 0) + half, 8), :] = zero_tile
    for half in (0, 8):
        cells[pl.ds(cell_row(-1, 7, 0, 0, 0) + half, 8), :] = zero_tile

    loads[0].wait()
    loads[1].wait()

    for x in range(8):
        field_w[0, x + 5, 8:16] = flag_v[x].astype(F32)
    exchanges = halo(0, field_w, field_out, field_in, FIELD_REACH)
    for load in loads[2:7]:
        load.wait()

    sub32 = iota((32, 128), 0)
    lane32 = iota((32, 128), 1)
    for xb in range(2):
        r0 = 32 * xb
        row = iota((32, 32), 0)
        column = iota((32, 32), 1)
        totals = count_v[xb].astype(F32)
        spread = jnp.where(
            (row & 1) == 0,
            jnp.broadcast_to(totals[0:1], (32, 32)),
            jnp.broadcast_to(totals[1:2], (32, 32)),
        )
        spread = jnp.where((column >> 1) == (row >> 1), spread, 0.0).astype(BF16)
        half = ((sub32 & 1) == (lane32 >> 6)).astype(F32).astype(BF16)
        live = jnp.dot(spread, half, preferred_element_type=F32)
        alive_v[pl.ds(r0, 32), :] = jnp.where(
            (lane32 & 63).astype(F32) < live, 1.0, 0.0
        )
        number_in_block = cell_v[pl.ds(r0, 32), :]
        bin_v[pl.ds(r0, 32), :] = (
            ((number_in_block >> 2) << 4)
            + (((sub32 >> 1) & 1) << 3)
            + ((lane32 >> 6) << 2)
            + (number_in_block & 3)
        )

    def deposit(step, carry):
        rows = pl.ds(pl.multiple_of(step * 16, 16), 16)
        alive = alive_v[rows, :]
        f = [off_v[d, rows, :] for d in range(3)]
        a = [aff_v[j, rows, :] for j in range(9)]
        base = [
            vel_v[k, rows, :] - (a[3 * k] * f[0] + a[3 * k + 1] * f[1] + a[3 * k + 2] * f[2])
            for k in range(3)
        ]
        hx = [(1.0 - f[0]) * alive, f[0] * alive]
        hy = [1.0 - f[1], f[1]]
        hz = [1.0 - f[2], f[2]]
        for ox in range(2):
            bx = [base[k] + a[3 * k] if ox else base[k] for k in range(3)]
            for oy in range(2):
                by = [bx[k] + a[3 * k + 1] if oy else bx[k] for k in range(3)]
                hxy = hx[ox] * hy[oy]
                for oz in range(2):
                    w = hxy * hz[oz]
                    channel = 16 * oz + 8 * ox + 4 * oy
                    start = pl.multiple_of(channel * 64 + step * 16, 16)
                    quant[pl.ds(start, 16), :] = w
                    for k in range(3):
                        bz = by[k] + a[3 * k + 2] if oz else by[k]
                        start = pl.multiple_of((channel + k + 1) * 64 + step * 16, 16)
                        quant[pl.ds(start, 16), :] = w * bz
        return carry

    lax.fori_loop(0, 4, deposit, 0)

    def bin_column(col, carry):
        xb, yb = col // 2, lax.rem(col, 2)
        first_z = (iota((16, 128), 1) & 15) == 0
        before = [0.0, 0.0]
        for pair in range(8):
            sides, hots = [], []
            for j in range(2):
                r = 32 * xb + yb + 4 * pair + 2 * j
                high, low = two_parts(quant[pl.ds(r, 32, stride=64), :])
                sides.append(jnp.concatenate([high, low], axis=0))
                hots.append(matches(bin_v[pl.ds(r, 1), :], 256))
            total = dot_last(jnp.concatenate(sides, axis=1), jnp.concatenate(hots, axis=1))
            total = total[0:32] + total[32:64]
            for h in range(2):
                lower = total[0:16, 128 * h : 128 * h + 128]
                upper = total[16:32, 128 * h : 128 * h + 128]
                carried = before[h]
                before[h] = pltpu.roll(upper, 113, 1)
                binned[2 * pair + h] = lower + jnp.where(
                    first_z, carried, pltpu.roll(upper, 1, 1)
                )
        for h in range(2):
            for g in range(2):
                parts = blocks_exchanged(
                    [binned[2 * pair + h, 8 * g : 8 * g + 8] for pair in range(8)]
                )
                for i in range(8):
                    q = 8 * h + i
                    start = ((4 * xb + q // 4 + 1) * 10 + 4 * yb + q % 4 + 1) * 16 + 8 * g
                    cells[pl.ds(pl.multiple_of(start, 8), 8), :] = parts[i]
        return carry

    lax.fori_loop(0, 4, bin_column, 0, unroll=4)

    for k in range(4):
        for x in range(9):
            total = None
            for ox in range(2):
                if not 0 <= x - ox < 8:
                    continue
                for oy in range(2):
                    part = cells[pl.ds(cell_row(x - ox, -oy, ox, oy, k), 8, stride=16), :]
                    total = part if total is None else total + part
            nodes[pl.ds((k * 9 + x) * 8, 8), :] = total
        column8[k] = (
            cells[pl.ds(cell_row(0, 7, 0, 1, k), 8, stride=160), :]
            + cells[pl.ds(cell_row(-1, 7, 1, 1, k), 8, stride=160), :]
        )

    def four(x, y, ox, oy):
        return cells[pl.ds(cell_row(x, y, ox, oy, 0), 4), :]

    corner88 = four(7, 7, 1, 1)
    d1 = jnp.concatenate([corner88, four(0, 7, 0, 1)], axis=0)
    d2 = jnp.concatenate([four(7, 0, 1, 0), four(0, 0, 0, 0)], axis=0)
    d3 = jnp.concatenate(
        [four(7, 7, 0, 1) + four(6, 7, 1, 1), four(7, 7, 1, 0) + four(7, 6, 1, 1)], axis=0
    )
    for k in range(4):
        message0[k] = nodes[pl.ds((k * 9 + 8) * 8, 8), :]
        message1[k] = nodes[pl.ds(k * 72, 8), :]
        message2[k] = column8[k]
        message3[k] = nodes[pl.ds(k * 72, 8, stride=8), :]
    for i, k in enumerate((0, 1)):
        message0[4 + i] = nodes[pl.ds((k * 9 + 7) * 8, 8), :]
    for i, k in enumerate((0, 2)):
        message2[4 + i] = nodes[pl.ds(k * 72 + 7, 8, stride=8), :]
    field_f = flat_rows(field_w)
    message0[6] = d1
    message1[4] = d1
    message2[6] = d1
    message3[4] = d2
    message0[7] = field_w[0, 12, 8:16]
    message1[5] = field_w[0, 5, 8:16]
    message2[7] = field_f[pl.ds(5 * 24 + 15, 8, stride=24), :]
    message3[5] = field_f[pl.ds(5 * 24 + 8, 8, stride=24), :]
    message4[0] = d1
    message4[1] = d3
    message7[0] = d2
    message7[1] = field_w[0, 5, 8:16]

    sums = [
        copy_to(number, 1, src, dst)
        for number, src, dst in (
            (0, message0, arrive0),
            (1, message1, arrive1),
            (2, message2, arrive2),
            (3, message3, arrive3),
            (4, message4, arrive4),
            (5, message7.at[pl.ds(0, 1)], arrive5),
            (6, message4.at[pl.ds(0, 1)], arrive6),
            (7, message7, arrive7),
        )
    ]
    pl.semaphore_wait(barrier, near_x * near_y - 1)
    for copy in sums:
        copy.start()

    for copy in exchanges:
        copy.start()

    loads[7].wait()
    loads[8].wait()

    def slot_rows(step, carry):
        for j in range(4):
            r = 4 * step + j
            slot = jnp.where(dest_v[pl.ds(r, 1), :] > 0, slot_v[pl.ds(r, 1), :], -1)
            lanes = pl.ds(pl.multiple_of(r * 128, 128), 128)
            slot_onehot[:, lanes] = matches(slot, 256)
        return carry

    lax.fori_loop(0, 16, slot_rows, 0)

    for copy in sums:
        copy.wait_recv()

    sub8 = iota((8, 128), 0)

    def at_first(v, row):
        return jnp.where(sub8 == 0, v + row, v)

    speed_f = speed_w.reshape(3 * 10 * 24, 128)

    def normalised(sums4, kind, dx, dy, components=(0, 1, 2)):
        inverse = 1.0 / jnp.maximum(sums4[0], MASS_FLOOR)
        result = []
        for k in components:
            u = sums4[k + 1] * inverse
            if k == 2:
                u = u - TIME_STEP * GRAVITY
            result.append(kept(jnp.where(kind == 2.0, 0.0, u), dx, dy))
        return result

    minus_rows, below_columns = [None] * 4, [None] * 4
    for i, k in enumerate((0, 1)):
        minus_rows[k] = at_first(
            kept(arrive0[4 + i], -1, 0), kept(arrive4[1, k : k + 1], -1, -1)
        )
    for i, k in enumerate((0, 2)):
        below_columns[k] = at_first(
            kept(arrive2[4 + i], 0, -1), kept(arrive4[1, 4 + k : 5 + k], -1, -1)
        )
    plus_rows, upper_columns = [], []
    for k in range(4):
        first = nodes[pl.ds(k * 72, 8), :] + kept(arrive0[k], -1, 0)
        nodes[pl.ds(k * 72, 8), :] = first
        column = at_first(
            kept(arrive2[k], 0, -1), kept(arrive4[0, k : k + 1], -1, -1)
        )
        nodes[pl.ds(k * 72, 8, stride=8), :] = (
            nodes[pl.ds(k * 72, 8, stride=8), :] + column
        )
        plus_rows.append(
            at_first(
                nodes[pl.ds((k * 9 + 8) * 8, 8), :] + kept(arrive1[k], 1, 0),
                kept(arrive2[6, k : k + 1], 0, -1)
                + kept(arrive6[0, 4 + k : 5 + k], 1, -1),
            )
        )
        upper_columns.append(
            at_first(
                column8[k] + kept(arrive3[k], 0, 1),
                kept(arrive0[6, k : k + 1], -1, 0) + kept(arrive5[0, k : k + 1], -1, 1),
            )
        )
    corner = (
        message4[0, 0:4]
        + kept(arrive1[4, 4:8], 1, 0)
        + kept(arrive3[4, 0:4], 0, 1)
        + kept(arrive7[0, 4:8], 1, 1)
    )

    for x in range(-1, 9):
        if x == -1:
            sums4, side = minus_rows, -1
        elif x == 8:
            sums4, side = plus_rows, 1
        else:
            sums4 = [nodes[pl.ds((k * 9 + x) * 8, 8), :] for k in range(4)]
            side = 0
        wanted = (0,) if x == -1 else (0, 1, 2)
        kind = {-1: arrive0[7], 1: arrive1[5], 0: field_w[0, x + 5, 8:16]}[side]
        u = normalised(sums4, kind, side, 0, wanted)
        for k in wanted:
            speed_w[k, x + 1, 8:16] = u[k]
    for columns, kind, y, side, wanted in (
        (below_columns, arrive2[7], 7, -1, (1,)),
        (upper_columns, arrive3[5], 16, 1, (0, 1, 2)),
    ):
        u = normalised(columns, kind, 0, side, wanted)
        for i, k in enumerate(wanted):
            speed_f[pl.ds((k * 10 + 1) * 24 + y, 8, stride=24), :] = u[i]
    u = normalised([corner[k : k + 1] for k in range(4)], arrive7[1, 0:1], 1, 1)
    for k in range(3):
        speed_w[k, 9, 16:17] = u[k]

    for x in range(8):
        source_w[0, x + 5, 8:16] = 0.5 * (
            speed_w[0, x + 2, 8:16]
            - speed_w[0, x, 8:16]
            + (speed_w[1, x + 1, 9:17] - speed_w[1, x + 1, 7:15])
            + (above_z(speed_w[2, x + 1, 8:16]) - below_z(speed_w[2, x + 1, 8:16]))
        )

    margins = halo(2, source_w, source_out, source_in, SOURCE_REACH)
    for copy in margins:
        copy.start()

    for copy in exchanges:
        copy.wait_recv()
    unpack(field_w, field_in, FIELD_REACH)

    sub24 = iota((24, 128), 0)
    ok_y = (
        jnp.where(sub24 < 8, inside_y[-1].astype(I32), 1)
        * jnp.where(sub24 >= 16, inside_y[1].astype(I32), 1)
    ) > 0
    for x in range(WIDE_X):
        side = -1 if x < 5 else 1 if x >= 13 else 0
        kind = kept(jnp.where(ok_y, field_w[0, x], 0.0), side, 0)
        solid_w[x, 8:32] = jnp.where(kind == 2.0, 1.0, 0.0)
        fluid = kind == 1.0
        scale_w[x] = jnp.where(fluid, 1.0, 0.0)
        press_a[x, 8:32] = jnp.where(fluid, field_w[1, x], 0.0)
    for x in range(1, WIDE_X - 1):
        middle = solid_w[x, 8:32]
        closed = (
            solid_w[x - 1, 8:32]
            + solid_w[x + 1, 8:32]
            + solid_w[x, 7:31]
            + solid_w[x, 9:33]
            + below_z(middle)
            + above_z(middle)
        )
        scale_w[x] = scale_w[x] / jnp.maximum(6.0 - closed, 1.0)

    for copy in margins:
        copy.wait_recv()
    unpack(source_w, source_in, SOURCE_REACH)

    old, new = press_a, press_b
    for sweep in range(ITERS):
        low, high = sweep + 1, WIDE_X - 1 - sweep
        for x in range(low, high):
            middle = old[x, 8:32]
            near = (
                old[x - 1, 8:32]
                + old[x + 1, 8:32]
                + old[x, 7:31]
                + old[x, 9:33]
                + below_z(middle)
                + above_z(middle)
            )
            scale = scale_w[x]
            new[x, 8:32] = jnp.where(scale > 0.0, scale * (near - source_w[0, x]), 0.0)
        old, new = new, old
    for x in range(8):
        press_o[x] = old[x + 5, 16:24]

    for x in range(9):
        w = x + 5
        p, s = old[w, 16:32], solid_w[w, 16:32]
        fluid = scale_w[w, 8:24] > 0.0
        slopes = (
            old[w + 1, 16:32]
            - old[w - 1, 16:32]
            + p * (solid_w[w + 1, 16:32] - solid_w[w - 1, 16:32]),
            old[w, 17:33]
            - old[w, 15:31]
            + p * (solid_w[w, 17:33] - solid_w[w, 15:31]),
            above_z(p) - below_z(p) + p * (above_z(s) - below_z(s)),
        )
        for k in range(3):
            settled[k, x] = speed_w[k, x + 1, 8:24] - jnp.where(fluid, 0.5 * slopes[k], 0.0)

    odd8 = (iota((8, 128), 0) & 1) == 1
    sub8 = iota((8, 128), 0)
    lane8 = iota((8, 128), 1)

    def table_row(k, ix, iy, j):
        return pl.ds(8 * (((k * 5 + ix) * 5 + iy) * 2 + j), 8)

    def sample_blocks(xb, carry):
        for k in range(3):
            for ix in range(5):
                for iy in range(5):
                    even = jnp.broadcast_to(settled[k, 4 * xb + ix, iy : iy + 1], (8, 128))
                    odd = jnp.broadcast_to(settled[k, 4 * xb + ix, iy + 4 : iy + 5], (8, 128))
                    table = jnp.where(odd8, odd, even)
                    tables[table_row(k, ix, iy, 0), :] = table
                    tables[table_row(k, ix, iy, 1), :] = above_z(table) - table
        return lax.fori_loop(0, 4, functools.partial(sample_rows, xb), carry, unroll=4)

    def sample_rows(xb, g, carry):
        start = pl.multiple_of(32 * xb + 8 * g, 8)
        rows = pl.ds(start, 8)
        cell = cell_v[rows, :]
        alive = alive_v[rows, :]
        qx, qy = cell >> 4, (cell >> 2) & 3
        z = ((4 * g + (sub8 >> 1)) << 3) + ((lane8 >> 6) << 2) + (cell & 3)
        at_x = [qx == i for i in range(4)]
        at_y = [qy == i for i in range(4)]
        f = [off_v[d, rows, :] for d in range(3)]

        def record_row(number):
            return pl.ds(pl.multiple_of(number * 64 + start, 8), 8)

        moving = dest_v[rows, :]

        def one_of(*numbers):
            hit = moving == numbers[0]
            for number in numbers[1:]:
                hit = hit | (moving == number)
            return jnp.where(hit, 8, 0)

        place = (
            4 * xb + qx - one_of(1, 5, 6) + one_of(2, 7, 8),
            ((sub8 & 1) << 2) + qy - one_of(3, 5, 7) + one_of(4, 6, 8),
            z,
        )
        for k in range(3):
            pick_x = [[None] * 4, [None] * 4]
            for ix in range(5):
                pick_y = [[None] * 2, [None] * 2]
                for iy in range(5):
                    got = [
                        jnp.take_along_axis(tables[table_row(k, ix, iy, j), :], z, axis=1)
                        for j in range(2)
                    ]
                    for o in range(2):
                        if not 0 <= iy - o < 4:
                            continue
                        for j in range(2):
                            held = pick_y[o][j]
                            pick_y[o][j] = (
                                got[j]
                                if held is None
                                else jnp.where(at_y[iy - o], got[j], held)
                            )
                flat = pick_y[0] + pick_y[1]
                for o in range(2):
                    if not 0 <= ix - o < 4:
                        continue
                    for j in range(4):
                        held = pick_x[o][j]
                        pick_x[o][j] = (
                            flat[j] if held is None else jnp.where(at_x[ix - o], flat[j], held)
                        )
            value, along_y, along_z = [], [], []
            for o in range(2):
                a0, rise0, a1, rise1 = pick_x[o]
                v0 = a0 + f[2] * rise0
                v1 = a1 + f[2] * rise1
                along_y.append(v1 - v0)
                value.append(v0 + f[1] * (v1 - v0))
                along_z.append(rise0 + f[1] * (rise1 - rise0))
            along_x = value[1] - value[0]
            speed = (value[0] + f[0] * along_x) * alive
            offset = f[k] + TIME_STEP * speed
            slope = (
                along_x * alive,
                (along_y[0] + f[0] * (along_y[1] - along_y[0])) * alive,
                (along_z[0] + f[0] * (along_z[1] - along_z[0])) * alive,
            )
            off_o[k, rows, :] = offset
            vel_o[k, rows, :] = speed
            records[record_row(k), :] = place[k].astype(F32) + offset
            records[record_row(3 + k), :] = speed
            for b in range(3):
                aff_o[3 * k + b, rows, :] = slope[b]
                records[record_row(6 + 3 * k + b), :] = slope[b]
        records[record_row(15), :] = jnp.zeros((8, 128), F32)
        for j in range(8):
            r = start + j
            record = records[pl.ds(r, 16, stride=64), :]
            high, low = two_parts(record)
            both = jnp.concatenate([high, low], axis=0)
            moving = jnp.broadcast_to(dest_v[pl.ds(r, 1), :].astype(F32), (32, 128)).astype(BF16)
            lanes = pl.ds(pl.multiple_of(r * 128, 128), 128)
            for number in range(8):
                hit = moving == jnp.full((32, 128), number + 1, BF16)
                parcels[pl.ds(32 * number, 32), lanes] = jnp.where(hit, both, jnp.zeros_like(both))
        return carry

    lax.fori_loop(0, 2, sample_blocks, 0)


    placed = dot_last(parcels[...], slot_onehot[...])
    leaving = [None] * 8
    for number in (4, 5, 6, 7, 0, 1, 2, 3):
        first = 32 * number
        outgoing[number] = placed[first : first + 16] + placed[first + 16 : first + 32]
        leaving[number] = copy_to(number, 3, outgoing.at[number], incoming.at[number])
        leaving[number].start()

    for copy in exchanges + sums + margins:
        copy.wait_send()

    rec_f = rec_o.reshape(15 * 16, 128)
    for number in (4, 5, 6, 7, 0, 1, 2, 3):
        leaving[number].wait_recv()
        leaving[number].wait_send()
        dx, dy = STEPS[number]
        arrived = kept(incoming[number], -dx, -dy)
        for half in range(2):
            rec_f[pl.ds(2 * number + half, 15, stride=16), :] = arrived[
                0:15, 128 * half : 128 * half + 128
            ]


def write_out(*refs):
    copies = [
        pltpu.make_async_copy(refs[i], refs[5 + i], refs[10].at[i]) for i in range(5)
    ]
    for copy in copies:
        copy.start()
    for copy in copies:
        copy.wait()


def in_rows(a):
    lead = a.shape[:-3]
    n = len(lead)
    turned = a.reshape(lead + (2, 2, 16, 128)).transpose(
        tuple(range(n)) + (n, n + 2, n + 1, n + 3)
    )
    return turned.reshape(lead + (64, 128))


def from_rows(a):
    lead = a.shape[:-2]
    n = len(lead)
    turned = a.reshape(lead + (2, 16, 2, 128)).transpose(
        tuple(range(n)) + (n, n + 2, n + 1, n + 3)
    )
    return turned.reshape(lead + (2, 2, 2048))


def on_device(
    nx,
    ny,
    cell_offset,
    velocity,
    affine,
    cell_index,
    counts,
    cell_flags,
    old_pressure,
    destination,
    dest_slot,
):
    vmem = pl.BlockSpec(memory_space=pltpu.VMEM)
    anywhere = pl.BlockSpec(memory_space=pltpu.HBM)

    def f32(*shape):
        return pltpu.VMEM(shape, F32)

    def halos(count, reach):
        rows = [8 * reach, 8 * (reach + 1)] + [8 * corner_tiles(n, reach) for n in range(4, 8)]
        return [f32(count, n, 128) for n in rows]

    shapes = ((3, 64, 128), (3, 64, 128), (9, 64, 128), (8, 8, 128), (15, 16, 128))
    outs = pl.pallas_call(
        functools.partial(kernel, nx, ny),
        out_shape=[pltpu.VMEM(shape, F32) for shape in shapes],
        in_specs=[anywhere] * 9,
        out_specs=[vmem] * 5,
        scratch_shapes=[
            f32(3, 64, 128),
            f32(3, 64, 128),
            f32(9, 64, 128),
            pltpu.VMEM((64, 128), I32),
            pltpu.VMEM((2, 2, 32), I32),
            pltpu.VMEM((64, 128), I32),
            pltpu.VMEM((64, 128), I32),
            pltpu.VMEM((8, 8, 128), I32),
            f32(2, WIDE_X, 24, 128),
            f32(64, 128),
            pltpu.VMEM((64, 128), I32),
            f32(32 * 64, 128),
            f32(16, 16, 128),
            f32(10 * 10 * 16, 128),
            f32(4 * 9 * 8, 128),
            f32(4, 8, 128),
            f32(8, 8, 128),
            f32(6, 8, 128),
            f32(8, 8, 128),
            f32(6, 8, 128),
            f32(2, 8, 128),
            f32(2, 8, 128),
        ]
        + [f32(tiles, 8, 128) for tiles in SUM_TILES]
        + [
            halos(2, FIELD_REACH),
            halos(2, FIELD_REACH),
            halos(1, SOURCE_REACH),
            halos(1, SOURCE_REACH),
            f32(3, 10, 24, 128),
            f32(1, WIDE_X, 24, 128),
            f32(WIDE_X, 24, 128),
            f32(WIDE_X, 40, 128),
            f32(WIDE_X, 40, 128),
            f32(WIDE_X, 40, 128),
            f32(3, 9, 16, 128),
            f32(150 * 8, 128),
            pltpu.VMEM((256, 8192), BF16),
            pltpu.VMEM((256, 8192), BF16),
            f32(16 * 64, 128),
            f32(8, 16, 256),
            f32(8, 16, 256),
            pltpu.SemaphoreType.DMA((9,)),
            pltpu.SemaphoreType.DMA((32,)),
            pltpu.SemaphoreType.DMA((32,)),
        ],
        compiler_params=pltpu.CompilerParams(
            collective_id=0, has_side_effects=True, vmem_limit_bytes=60 * 1024 * 1024
        ),
        name="substep",
    )(
        *[
            pltpu.with_memory_space_constraint(a, pltpu.HBM)
            for a in (
                in_rows(cell_offset),
                in_rows(velocity),
                in_rows(affine),
                in_rows(cell_index),
                counts,
                cell_flags,
                old_pressure,
                in_rows(destination),
                in_rows(dest_slot),
            )
        ]
    )
    outs = pl.pallas_call(
        write_out,
        out_shape=[jax.ShapeDtypeStruct(shape, F32) for shape in shapes],
        in_specs=[vmem] * 5,
        out_specs=[anywhere] * 5,
        scratch_shapes=[pltpu.SemaphoreType.DMA((5,))],
        compiler_params=pltpu.CompilerParams(vmem_limit_bytes=60 * 1024 * 1024),
        name="write_out",
    )(*[pltpu.with_memory_space_constraint(a, pltpu.VMEM) for a in outs])
    return (
        from_rows(outs[0]),
        from_rows(outs[1]),
        from_rows(outs[2]),
        outs[3],
        outs[4].reshape(15, 8, 1, 256),
    )


def solution(mesh):
    particles, blocks = P(None, "gx", "gy", None), P("gx", "gy", None)
    return jax.shard_map(
        functools.partial(on_device, mesh.shape["gx"], mesh.shape["gy"]),
        mesh=mesh,
        in_specs=(particles, particles, particles) + (blocks,) * 6,
        out_specs=(particles, particles, particles, blocks, P(None, None, "gx", "gy")),
        check_vma=False,
    )
```
